512 devices in a mesh: ctx: 64 (over x, z, core), tp: 8 (over y).
Axes of the slice: x: 4, y: 8, z: 8, core: 2. Of those that a mesh axis runs over, the one named last changes fastest.
Arguments:
- features: bfloat16 [128, 196, 1152], P('ctx', None, 'tp'), may hold values from -6 to 6
- group_kernel: bfloat16 [9, 1152, 48], P(None, 'tp'), may hold values from -0.3125 to 0.3125
- squeeze_in: bfloat16 [1152, 288], P('tp'), may hold values from -0.75 to 0.75
- squeeze_out: bfloat16 [288, 1152], P(None, 'tp'), may hold values from -0.75 to 0.75
- sampler_kernel: bfloat16 [1152, 8, 1152], P('ctx', None, 'tp'), may hold values from -0.0625 to 0.0625
- readout_kernel: bfloat16 [1152, 8192], P('ctx', 'tp'), may hold values from -0.1875 to 0.1875
- frame_clip: int32 [128], replicated, may hold values from 0 to 15, as said below
- clip_keep: int32 [16], replicated, may hold values from 1 to 512, as said below
- token_cotangent: bfloat16 [4096, 8192], P('ctx', 'tp'), may hold values from -6 to 6
Outputs:
- llm_tokens: bfloat16 [4096, 8192], P('ctx', 'tp')
- grad_features: bfloat16 [128, 196, 1152], P('ctx', None, 'tp')
The draws below stay inside these ranges and needn't reach their ends.
Inputs may be any that keep to these rules, and one draw needn't show every extreme that they name: `frame_clip`: clip ids start at 0 and never fall along the frames; every clip covers an even number of frames from 2 to 16 and starts at an even frame; some clip covers 16. `clip_keep`: each clip keeps at least one and at most 8 * 8 times half its frames of its tokens; the clip of 16 frames keeps all of its tokens, and some clip keeps a single token.
All inputs are finite; a program needn't handle non-finite values.
Results may differ from the reference program's by a relative error of at most 0.009.
Values may be sent and summed in bfloat16 or wider, within the bound.
A program may use at most 64 MiB of HBM per device.

```python
import jax
import jax.numpy as jnp
from jax import lax

C = 1152
H = 8192
G = 48
SIDE = 14
R = 288
OUT_SIDE = 8
CELLS = 196
FRAMES = 128
CLIPS = 16
TOKENS = 4096
N_CTX = 64


def clip_order(key):
    return jax.random.permutation(jax.random.fold_in(key, 9), CLIPS)


def clip_lengths(key):
    halves = jax.random.randint(jax.random.fold_in(key, 7), (CLIPS // 2,), -3, 4)
    paired = jnp.stack([4 + halves, 4 - halves], axis=1).reshape(CLIPS).astype(jnp.int32)
    fixed_head = jnp.array([8, 2, 3, 3], dtype=jnp.int32)
    joined = jnp.concatenate([fixed_head, paired[4:]])
    return joined[clip_order(key)]


def clip_marks(key):
    fixed_head = jnp.array([2, 1, 0, 0], dtype=jnp.int32)
    joined = jnp.concatenate([fixed_head, jnp.zeros((CLIPS - 4,), jnp.int32)])
    return joined[clip_order(key)]


def pair_clips(key):
    lengths = clip_lengths(key)
    ends = jnp.cumsum(lengths)
    slots = jnp.arange(FRAMES // 2, dtype=jnp.int32)
    return jnp.sum((ends[None, :] <= slots[:, None]).astype(jnp.int32), axis=1).astype(jnp.int32)


def draw_frame_clip(key, part):
    return jnp.repeat(pair_clips(key), 2).astype(jnp.int32)


def draw_clip_keep(key, part):
    produced = clip_lengths(key) * (OUT_SIDE * OUT_SIDE)
    marks = clip_marks(key)
    picked = jax.random.randint(jax.random.fold_in(key, 11), (CLIPS,), 1, 2 * produced)
    kept = jnp.minimum(picked, produced)
    kept = jnp.where(marks == 2, produced, kept)
    kept = jnp.where(marks == 1, jnp.ones_like(kept), kept)
    return kept.astype(jnp.int32)


def shard_levels(key, shape, cuts, low, largest):
    def one(dim, blocks):
        steps = jax.random.uniform(jax.random.fold_in(jax.random.fold_in(key, 6), dim), (blocks,), jnp.float32, low / len(cuts), largest / len(cuts))
        return jnp.repeat(jnp.exp(steps), shape[dim] // blocks).reshape((-1,) + (1,) * (len(shape) - dim - 1))

    factor_of = one(*cuts[0])
    for cut in cuts[1:]:
        factor_of = factor_of * one(*cut)
    return factor_of


def bell_draw(own_key, shape, scale, reach, pieces=(), held_as=jnp.bfloat16):
    values = scale * jax.random.normal(own_key, shape, jnp.float32)
    if pieces:
        values = values * shard_levels(own_key, shape, pieces, -0.22, 0.18)
    return jnp.clip(values, -reach, reach).astype(held_as)


def setup_inputs(seed: int = 0) -> dict:
    key_list = jax.random.split(jax.random.key(seed), 10)
    return {
        "features": bell_draw(key_list[0], (FRAMES, CELLS, C), 1.0, 6.0, ((0, 64), (2, 8))),
        "group_kernel": bell_draw(key_list[1], (9, C, G), (9 * G) ** -0.5, 0.3125, ((1, 8),)),
        "squeeze_in": bell_draw(key_list[2], (C, R), (C // 16) ** -0.5, 0.75, ((0, 8),)),
        "squeeze_out": bell_draw(key_list[3], (R, C), (R // 4) ** -0.5, 0.75, ((1, 8),)),
        "sampler_kernel": bell_draw(key_list[4], (C, 8, C), (8 * C) ** -0.5, 0.0625, ((0, 64), (2, 8))),
        "readout_kernel": bell_draw(key_list[5], (C, H), C ** -0.5, 0.1875, ((0, 64), (1, 8))),
        "frame_clip": draw_frame_clip(jax.random.fold_in(key_list[9], 71), 0),
        "clip_keep": draw_clip_keep(jax.random.fold_in(key_list[9], 71), 0),
        "token_cotangent": bell_draw(key_list[8], (TOKENS, H), 1.0, 6.0, ((0, 64), (1, 8))),
    }


def silu_slope(values):
    sigma = jax.nn.sigmoid(values)
    return sigma * (1.0 + values * (1.0 - sigma))


def grouped_forward(frames_grid, group_kernel):
    count, side, _, chans = frames_grid.shape
    width = group_kernel.shape[2]
    groups = chans // width
    padded = jnp.pad(frames_grid, ((0, 0), (1, 1), (1, 1), (0, 0)))
    kernel = group_kernel.reshape(9, groups, width, width).astype(jnp.float32)
    total = jnp.zeros((count, side, side, groups, width), jnp.float32)
    for kernel_tap in range(9):
        row_shift, col_shift = divmod(kernel_tap, 3)
        window = padded[:, row_shift:row_shift + side, col_shift:col_shift + side]
        window = window.reshape(count, side, side, groups, width).astype(jnp.float32)
        total = total + jnp.einsum("fyxgi,gio->fyxgo", window, kernel[kernel_tap])
    return total.reshape(count, side, side, chans)


def grouped_backward(grad_grid, group_kernel):
    count, side, _, chans = grad_grid.shape
    width = group_kernel.shape[2]
    groups = chans // width
    kernel = group_kernel.reshape(9, groups, width, width).astype(jnp.float32)
    source = grad_grid.reshape(count, side, side, groups, width).astype(jnp.float32)
    total = jnp.zeros((count, side + 2, side + 2, chans), jnp.float32)
    for kernel_tap in range(9):
        row_shift, col_shift = divmod(kernel_tap, 3)
        spread = jnp.einsum("fyxgo,gio->fyxgi", source, kernel[kernel_tap]).reshape(count, side, side, chans)
        total = total + jnp.pad(spread, ((0, 0), (row_shift, 2 - row_shift), (col_shift, 2 - col_shift), (0, 0)))
    return total[:, 1:side + 1, 1:side + 1]


def make_patches(prev_odd, even):
    stacked = jnp.stack([prev_odd, even], axis=1)
    stacked = jnp.pad(stacked, ((0, 0), (0, 0), (1, 1), (1, 1), (0, 0)))
    pairs, _, padded_side, _, chans = stacked.shape
    half = padded_side // 2
    shaped = stacked.reshape(pairs, 2, half, 2, half, 2, chans).transpose(0, 2, 4, 1, 3, 5, 6)
    return shaped.reshape(pairs * half * half, 8 * chans)


def unpatch(grad_rows, pairs, side, chans):
    half = side // 2 + 1
    shaped = grad_rows.reshape(pairs, half, half, 2, 2, 2, chans).transpose(0, 3, 1, 4, 2, 5, 6)
    shaped = shaped.reshape(pairs, 2, 2 * half, 2 * half, chans)
    return shaped[:, :, 1:side + 1, 1:side + 1]


def reorder(rows):
    width = rows.shape[1]
    return rows.reshape(N_CTX, N_CTX, -1, width).transpose(1, 0, 2, 3).reshape(-1, width)


def reference(features, group_kernel, squeeze_in, squeeze_out, sampler_kernel, readout_kernel, frame_clip, clip_keep, token_cotangent):
    highest = lax.Precision.HIGHEST
    frames, cells, chans = features.shape
    pairs = frames // 2
    grid = features.reshape(frames, SIDE, SIDE, chans)
    conv_out = grouped_forward(grid, group_kernel)
    active = jax.nn.silu(conv_out)
    pooled = jnp.mean(active, axis=(1, 2))
    squeezed = jnp.dot(pooled, squeeze_in.astype(jnp.float32), precision=highest)
    relaxed = jax.nn.silu(squeezed)
    excite = jax.nn.sigmoid(jnp.dot(relaxed, squeeze_out.astype(jnp.float32), precision=highest))
    hidden = (grid.astype(jnp.float32) + active * excite[:, None, None, :]).astype(jnp.bfloat16)
    same_clip = frame_clip[1:-1:2] == frame_clip[2::2]
    pair_mask = jnp.concatenate([jnp.zeros((1,), bool), same_clip]).astype(jnp.float32)
    even = hidden[0::2]
    odd = hidden[1::2]
    prev_odd = jnp.concatenate([jnp.zeros_like(odd[:1]), odd[:-1]], axis=0)
    prev_odd = prev_odd * pair_mask.astype(jnp.bfloat16)[:, None, None, None]
    patches = make_patches(prev_odd, even)
    sampler_rows = sampler_kernel.reshape(chans, 8 * chans)
    pre = jnp.dot(patches, sampler_rows.T, preferred_element_type=jnp.float32)
    act = jax.nn.silu(pre).astype(jnp.bfloat16)
    per_frame = OUT_SIDE * OUT_SIDE
    pair_clip = frame_clip[0::2]
    clip_ids = jnp.arange(clip_keep.shape[0], dtype=jnp.int32)
    start_pair = jnp.sum((pair_clip[None, :] < clip_ids[:, None]).astype(jnp.int32), axis=1)
    own_start = start_pair[pair_clip]
    own_keep = clip_keep[pair_clip]
    pair_index = jnp.arange(pairs, dtype=jnp.int32)
    position = (pair_index - own_start)[:, None] * per_frame + jnp.arange(per_frame, dtype=jnp.int32)[None, :]
    live = (position < own_keep[:, None]).reshape(-1).astype(jnp.bfloat16)
    tokens = jnp.dot(act, readout_kernel, preferred_element_type=jnp.float32).astype(jnp.bfloat16) * live[:, None]
    llm_tokens = reorder(tokens)
    back = reorder(token_cotangent) * live[:, None]
    grad_act = jnp.dot(back, readout_kernel.T, preferred_element_type=jnp.float32)
    grad_pre = (grad_act * silu_slope(pre)).astype(jnp.bfloat16)
    grad_patches = jnp.dot(grad_pre, sampler_rows, preferred_element_type=jnp.float32)
    grad_taps = unpatch(grad_patches, pairs, SIDE, chans)
    leading = grad_taps[:, 0] * pair_mask[:, None, None, None]
    grad_even = grad_taps[:, 1]
    grad_odd = jnp.concatenate([leading[1:], jnp.zeros_like(leading[:1])], axis=0)
    grad_hidden = jnp.stack([grad_even, grad_odd], axis=1).reshape(frames, SIDE, SIDE, chans)
    grad_excite = jnp.sum(grad_hidden * active, axis=(1, 2))
    grad_inner = grad_excite * excite * (1.0 - excite)
    grad_relaxed = jnp.dot(grad_inner, squeeze_out.astype(jnp.float32).T, precision=highest)
    grad_squeezed = grad_relaxed * silu_slope(squeezed)
    grad_pooled = jnp.dot(grad_squeezed, squeeze_in.astype(jnp.float32).T, precision=highest)
    grad_active = grad_hidden * excite[:, None, None, :] + grad_pooled[:, None, None, :] / cells
    grad_conv = (grad_active * silu_slope(conv_out)).astype(jnp.bfloat16)
    grad_grid = grad_hidden + grouped_backward(grad_conv, group_kernel)
    grad_features = grad_grid.astype(jnp.bfloat16).reshape(frames, cells, chans)
    return llm_tokens, grad_features
```

```python
import jax
import jax.numpy as jnp
from jax import lax
from jax.experimental import pallas as pl
from jax.experimental.pallas import tpu as pltpu
from jax.sharding import PartitionSpec as P

NX, NZ, NT = 4, 8, 8
BF = jnp.bfloat16
F32 = jnp.float32
MESH = pl.DeviceIdType.MESH
SLOT = (0, 128, 256, 384, 640, 768, 896, 1024)


def iota(shape, dim):
    return lax.broadcasted_iota(jnp.int32, shape, dim)


def select(hit):
    return jnp.where(hit, 1.0, 0.0).astype(BF)


def mm(a, b):
    return jnp.dot(a, b, preferred_element_type=F32)


def mmt(a, b):
    return lax.dot_general(a, b, (((1,), (1,)), ((), ())), preferred_element_type=F32)


def exact(dot, value, weight):
    high = value.astype(BF)
    left = value - high.astype(F32)
    middle = left.astype(BF)
    low = (left - middle.astype(F32)).astype(BF)
    return dot(high, weight) + (dot(middle, weight) + dot(low, weight))


def sigmoid(v):
    return jax.nn.sigmoid(v)


def slope(v):
    s = sigmoid(v)
    return s * (1.0 + v * (1.0 - s))


def padded_place(cell):
    row = (cell * 4682) >> 16
    return (row + 1) * 16 + (cell - 14 * row) + 1


def patch_place(r):
    s = r >> 6
    a = (r >> 3) & 7
    b = r & 7
    return (2 * a + (s >> 1)) * 16 + 2 * b + (s & 1)


def third(v):
    return (v >= 48).astype(jnp.int32) + (v >= 96).astype(jnp.int32)


def kernel(
    feat, gk, sqi, sqo, samp, read, fclip, keep, cot,
    llm, gout,
    sall, rall, srest, rrest, fta, ftb, cotb, wc, xs, cv, ac, sl, bm, gh, sqie, sqoe, pbuf, psl, psl2,
    p0, p1, obuf, prep, rsp, gap, rsg, gas, gad, acs, acd, gpf, acf, gpt, ges, ger, gos, gor, tks, tkr,
    cot_sem, sx_s, sx_r, sz_s, sz_r, sh_r, rz_s, rz_r, rx_s, rx_r, rh_r, ps_s, ps_r, pq_s, pq_r,
    e_sem, o_s, o_r, rp_s, rp_r, rg_s, rg_r, ga_s, ga_r, aa_s, aa_r, gp_s, gp_r, af_s, af_r,
    ge_sem, go_s, go_r, tk_sem,
):
    ctx = lax.axis_index("ctx")
    t = lax.axis_index("tp")
    k = lax.rem(ctx, 2)
    m = lax.div(ctx, 2)
    z = lax.rem(m, NZ)
    x = lax.div(m, NZ)
    chips = NX * NZ

    def dev(xx, zz, kk, tt):
        return ((xx * NZ + zz) * 2 + kk, tt)

    def chip(mm_, kk):
        return (lax.rem(mm_ + chips, chips) * 2 + kk, t)

    def zdev(d):
        return dev(x, lax.rem(z + d + NZ, NZ), k, t)

    def xdev(d):
        return dev(lax.rem(x + d + NX, NX), z, k, t)

    def tdev(d):
        return (ctx, lax.rem(t + d, NT))

    sibling = (m * 2 + (1 - k), t)
    t_low, t_high = lax.rem(t, 4), lax.div(t, 4)
    row_slot = 2 * z + t_high
    is_self = (t_low == x).astype(jnp.int32)

    def row_dev(i):
        return dev(t_low, i // 2, k, (i % 2) * 4 + x)

    def remote(src, dst, send, recv, where):
        return pltpu.make_async_remote_copy(
            src_ref=src, dst_ref=dst, send_sem=send, recv_sem=recv, device_id=where, device_id_type=MESH
        )

    sent = []

    def start(copy):
        copy.start()
        sent.append(copy)

    barrier = pltpu.get_barrier_semaphore()

    def hello(where):
        pl.semaphore_signal(barrier, inc=1, device_id=where, device_id_type=MESH)

    hello(sibling)
    for d in range(1, NX):
        hello(xdev(d))
    for d in range(1, NZ):
        hello(zdev(d))
    for d in range(1, NT):
        hello(tdev(d))
    hello(chip(m - 1, 1))

    @pl.when(k == 1)
    def _():
        hello(chip(m + 1, 0))
        hello(chip(m + 1, 1))

    for i in range(16):
        @pl.when(jnp.logical_not(jnp.logical_and(is_self == 1, row_slot == i)))
        def _(i=i):
            hello(row_dev(i))

    ftb[0:144, :] = jnp.zeros((144, 128), F32)
    fta[0:144, :] = samp[:, 0:128].astype(F32)
    ftb[0:144, 0:16] = samp[:, 128:144].astype(F32)
    rest = jnp.zeros((16, 128), F32)
    for s in range(8):
        sall[z, x, :, SLOT[s] : SLOT[s] + 128] = fta[pl.ds(s, 16, stride=8), :].astype(BF)
        tail = ftb[pl.ds(s, 16, stride=8), :]
        rest = rest + (tail if s == 0 else pltpu.roll(tail, 16 * s, 1))
    sall[z, x, :, 512:640] = rest.astype(BF)
    sall[z, x, :, 1152:1280] = fta[128:144, :].astype(BF)
    sall[z, x, :, 1280:1408] = ftb[128:144, :].astype(BF)
    rall[z, x, :, 0:1024] = read[0:16, :]
    last = read[16:18, :].astype(F32)
    for j in range(2):
        for p in range(8):
            fta[256 + j * 8 + p : 257 + j * 8 + p, :] = last[j : j + 1, 128 * p : 128 * p + 128]
    rall[z, x, :, 1024:1152] = fta[256:272, :].astype(BF)

    pl.semaphore_wait(barrier, 1 + (NX - 1) + (NZ - 1) + (NT - 1) + (1 + 2 * k) + 16 - is_self)

    for d in range(1, NX):
        start(remote(sall.at[z, x], sall.at[z, x], sx_s.at[d], sx_r.at[x], xdev(d)))
    for d in range(1, NZ):
        start(remote(rall.at[z, x], rall.at[z, x], rz_s.at[d], rz_r.at[z], zdev(d)))
    start(remote(cot, cotb.at[k], cot_sem.at[0], cot_sem.at[1], sibling))
    cotb[k] = cot[...]

    def wait_sx():
        for d in range(1, NX):
            o = lax.rem(x + d, NX)
            remote(sall.at[z, o], sall.at[z, o], sx_s.at[d], sx_r.at[o], xdev(d)).wait_recv()

    def zi(d):
        return lax.rem(z + d + 2 * NZ, NZ)

    def ring_s(i):
        up, down = zi(1 - i), zi(i - 1)
        if i < 4:
            start(remote(sall.at[up], sall.at[up], sz_s.at[i], sz_r.at[up], zdev(1)))
            start(remote(sall.at[down], sall.at[down], sz_s.at[i + 4], sz_r.at[down], zdev(-1)))
        else:
            start(remote(sall.at[up, 0:2], sall.at[up, 0:2], sz_s.at[4], sh_r.at[0], zdev(1)))
            start(remote(sall.at[down, 2:4], sall.at[down, 2:4], sz_s.at[8], sh_r.at[1], zdev(-1)))

    def wait_ring_s(i):
        up, down = zi(-i), zi(i)
        if i < 4:
            remote(sall.at[up], sall.at[up], sz_s.at[i], sz_r.at[up], zdev(1)).wait_recv()
            remote(sall.at[down], sall.at[down], sz_s.at[i + 4], sz_r.at[down], zdev(-1)).wait_recv()
        else:
            remote(sall.at[up, 0:2], sall.at[up, 0:2], sz_s.at[4], sh_r.at[0], zdev(1)).wait_recv()
            remote(sall.at[down, 2:4], sall.at[down, 2:4], sz_s.at[8], sh_r.at[1], zdev(-1)).wait_recv()

    def wait_rz():
        for d in range(1, NZ):
            o = zi(d)
            remote(rall.at[o, x], rall.at[o, x], rz_s.at[d], rz_r.at[o], zdev(d)).wait_recv()

    def xi(d):
        return lax.rem(x + d + NX, NX)

    def r_x(i):
        if i == 1:
            start(remote(rall.at[:, x], rall.at[:, x], rx_s.at[0], rx_r.at[0], xdev(1)))
            start(remote(rall.at[:, x], rall.at[:, x], rx_s.at[1], rx_r.at[1], xdev(-1)))
        else:
            up, down = xi(-1), xi(1)
            start(remote(rall.at[0:4, up], rall.at[0:4, up], rx_s.at[2], rh_r.at[0], xdev(1)))
            start(remote(rall.at[4:8, down], rall.at[4:8, down], rx_s.at[3], rh_r.at[1], xdev(-1)))

    def wait_r_x(i):
        if i == 1:
            up, down = xi(-1), xi(1)
            remote(rall.at[:, up], rall.at[:, up], rx_s.at[0], rx_r.at[0], xdev(1)).wait_recv()
            remote(rall.at[:, down], rall.at[:, down], rx_s.at[1], rx_r.at[1], xdev(-1)).wait_recv()
        else:
            far = xi(2)
            remote(rall.at[0:4, far], rall.at[0:4, far], rx_s.at[2], rh_r.at[0], xdev(1)).wait_recv()
            remote(rall.at[4:8, far], rall.at[4:8, far], rx_s.at[3], rh_r.at[1], xdev(-1)).wait_recv()

    widen = select(jnp.logical_and(iota((144, 256), 0) == iota((144, 256), 1), iota((144, 256), 1) < 144))
    cell = iota((256, 256), 0)
    cy, cx = cell >> 4, cell & 15
    inside = jnp.logical_and(
        jnp.logical_and(cy >= 1, cy <= 14), jnp.logical_and(cx >= 1, cx <= 14)
    )
    bm[...] = jnp.where(inside, 1.0, 0.0)
    into = select(padded_place(iota((256, 196), 1)) == iota((256, 196), 0))
    column = iota((48, 256), 1)
    spread = select(jnp.logical_and(column - 48 * third(column) == iota((48, 256), 0), column < 144))
    same_group = third(iota((144, 256), 0)) == third(iota((144, 256), 1))

    def centre(f):
        wide = mm(feat[f], widen).astype(BF)
        return mm(into, wide)

    def put_shifts(f, value):
        xs[f, 0, 16:272, :] = pltpu.roll(value, 1, 0).astype(BF)
        xs[f, 1, 16:272, :] = value.astype(BF)
        xs[f, 2, 16:272, :] = pltpu.roll(value, 255, 0).astype(BF)

    for f in range(2):
        for j in range(3):
            xs[f, j, 0:16, :] = jnp.zeros((16, 256), BF)
            xs[f, j, 272:288, :] = jnp.zeros((16, 256), BF)
        put_shifts(f, centre(f))
    for tap in range(9):
        dense = jnp.where(same_group, mm(gk[tap], spread), 0.0)
        wc[tap, 0:144, :] = dense.astype(BF)
        wc[tap, 144:256, :] = jnp.zeros((112, 256), BF)
    sqoe[...] = mm(sqo[...], widen).astype(BF)
    sqie[0:144, :] = sqi[...]
    sqie[144:256, :] = jnp.zeros((112, 288), BF)
    pbuf[...] = jnp.zeros((8, 256), F32)

    wait_sx()
    ring_s(1)

    def conv(f):
        total = jnp.zeros((256, 256), F32)
        for dy in range(3):
            for dx in range(3):
                total = total + mm(xs[f, dx, 16 * dy : 16 * dy + 256, :], wc[3 * dy + dx])
        cv[f] = total
        act = total * sigmoid(total) * bm[...]
        ac[f] = act
        pbuf[f : f + 1, :] = jnp.sum(act, axis=0, keepdims=True) * (1.0 / 196.0)

    conv(0)
    conv(1)
    psl[t] = exact(mm, pbuf[...], sqie[...])
    for d in range(1, NT):
        start(remote(psl.at[t], psl.at[t], ps_s.at[d], ps_r.at[t], tdev(d)))

    wait_rz()
    r_x(1)

    clips = fclip[...].astype(F32)
    lane = iota((64, 128), 1)
    row = iota((64, 128), 0)
    clip_col = jnp.sum(jnp.where(lane == 2 * row, clips, 0.0), axis=1, keepdims=True)
    before = jnp.logical_and((lane & 1) == 0, clips < clip_col)
    first = jnp.sum(jnp.where(before, 1.0, 0.0), axis=1, keepdims=True)
    lane16 = iota((64, 16), 1).astype(F32)
    kept = jnp.sum(jnp.where(lane16 == clip_col, keep[...].astype(F32), 0.0), axis=1, keepdims=True)
    place = (iota((64, 1), 0).astype(F32) - first) * 64.0

    def live(d):
        return jnp.where(place + jnp.asarray(d, jnp.int32).astype(F32) < kept, 1.0, 0.0)

    lane1 = iota((1, 128), 1)

    def pair_mask(c):
        now = jnp.sum(jnp.where(lane1 == 2 * c, clips, 0.0), axis=1, keepdims=True)
        was = jnp.sum(jnp.where(lane1 == 2 * c - 1, clips, 0.0), axis=1, keepdims=True)
        return jnp.where(jnp.logical_and(now == was, iota((1, 1), 0) + c > 0), 1.0, 0.0)

    mask0, mask1 = pair_mask(2 * m), pair_mask(2 * m + 1)

    for f in range(2):
        sl[f] = slope(cv[f]) * bm[...]

    def wait_slots(slots, send, recv):
        for d in range(1, NT):
            o = lax.rem(t + d, NT)
            remote(slots.at[o], slots.at[o], send.at[d], recv.at[o], tdev(d)).wait_recv()

    wait_slots(psl, ps_s, ps_r)
    squeezed = jnp.sum(psl[...], axis=0)
    excite = sigmoid(exact(mm, squeezed * sigmoid(squeezed), sqoe[...]))
    gather = select(patch_place(iota((256, 256), 0)) == iota((256, 256), 1))
    for f in range(2):
        hidden = xs[f, 1, 16:272, :].astype(F32) + ac[f] * excite[f : f + 1, :]
        taps = mm(gather, hidden.astype(BF))
        base = 4 * (1 - f)
        rest = jnp.zeros((64, 128), F32)
        for s in range(4):
            tail = taps[64 * s : 64 * s + 64, 128:256]
            by = 16 * (s + base)
            rest = rest + (tail if by == 0 else pltpu.roll(tail, by, 1))
        main = taps[:, 0:128].astype(BF)
        if f == 0:
            mine = pl.ds(pl.multiple_of(64 * k, 64), 64)
            p1[mine, 0:128] = rest.astype(BF)
            for s in range(4):
                p1[mine, 128 * (s + 1) : 128 * (s + 2)] = main[64 * s : 64 * s + 64]
            start(remote(p1.at[mine], p1.at[mine], e_sem.at[0], e_sem.at[1], sibling))
        else:
            obuf[:, 512:640] = rest.astype(BF)
            for s in range(4):
                obuf[:, 128 * s : 128 * (s + 1)] = main[64 * s : 64 * s + 64]

    @pl.when(k == 0)
    def _():
        p0[64:128, :] = obuf[...]
        remote(obuf, p0.at[64:128], o_s.at[0], o_r.at[1], sibling).start()

    @pl.when(k == 1)
    def _():
        remote(obuf, p0.at[0:64], o_s.at[0], o_r.at[0], chip(m + 1, 1)).start()
        remote(obuf, p0.at[0:64], o_s.at[1], o_r.at[0], chip(m + 1, 0)).start()

    wait_ring_s(1)
    ring_s(2)
    wait_r_x(1)
    r_x(2)
    wait_ring_s(2)
    ring_s(3)

    other = pl.ds(pl.multiple_of(64 * (1 - k), 64), 64)
    wait_r_x(2)
    fta[...] = rall[:, :, :, 1024:1152].reshape(512, 128).astype(F32)
    for p in range(8):
        rrest[0:64, 128 * p : 128 * p + 128] = fta[pl.ds(p, 64, stride=8), :].astype(BF)
    rrest[64:128, :] = jnp.zeros((64, 1024), BF)
    remote(cot, cotb.at[1 - k], cot_sem.at[0], cot_sem.at[1], sibling).wait_recv()
    back = cotb[...].reshape(128, 1024)
    alive = jnp.concatenate([live(2 * m), live(2 * m + 1)], axis=0)
    gap[:, :, 0:512] = (
        (mmt(back, rall[:, :, :, 0:1024].reshape(512, 1024)) * alive).astype(BF).reshape(8, 16, 512)
    )
    gap[:, :, 512:640] = (mmt(back, rrest[...]) * alive).astype(BF).reshape(8, 16, 128)

    def scatter(parts, slots, send, recv):
        for d in range(1, NT):
            o = lax.rem(t + d, NT)
            start(remote(parts.at[o], slots.at[t], send.at[d], recv.at[t], tdev(d)))

    def scattered(parts, slots, send, recv):
        wait_slots(slots, send, recv)
        total = parts[t].astype(F32)
        for d in range(1, NT):
            total = total + slots[lax.rem(t + d, NT)].astype(F32)
        return total

    scatter(gap, rsg, rg_s, rg_r)

    wait_ring_s(3)
    ring_s(4)

    remote(p1.at[other], p1.at[other], e_sem.at[0], e_sem.at[1], sibling).wait_recv()
    remote(obuf, p0.at[0:64], o_s.at[0], o_r.at[0], sibling).wait_recv()

    @pl.when(k == 1)
    def _():
        remote(obuf, p0.at[64:128], o_s.at[0], o_r.at[1], sibling).wait_recv()

    wait_ring_s(4)
    fta[...] = sall[:, :, :, 1152:1280].reshape(512, 128).astype(F32)
    ftb[...] = sall[:, :, :, 1280:1408].reshape(512, 128).astype(F32)
    rest = jnp.zeros((64, 128), F32)
    for s in range(8):
        srest[0:64, SLOT[s] : SLOT[s] + 128] = fta[pl.ds(s, 64, stride=8), :].astype(BF)
        tail = ftb[pl.ds(s, 64, stride=8), :]
        rest = rest + (tail if s == 0 else pltpu.roll(tail, 16 * s, 1))
    srest[0:64, 512:640] = rest.astype(BF)
    srest[64:128, :] = jnp.zeros((64, 1152), BF)

    mask_col = jnp.concatenate(
        [jnp.broadcast_to(mask0, (64, 1)), jnp.broadcast_to(mask1, (64, 1))], axis=0
    )

    def pre_part(w0, w1):
        return mmt(p0[...], w0) * mask_col + mmt(p1[...], w1)

    prep[:, :, 0:512] = (
        pre_part(sall[:, :, :, 0:640].reshape(512, 640), sall[:, :, :, 512:1152].reshape(512, 640))
        .astype(BF)
        .reshape(8, 16, 512)
    )
    prep[:, :, 512:640] = pre_part(srest[:, 0:640], srest[:, 512:1152]).astype(BF).reshape(8, 16, 128)
    scatter(prep, rsp, rp_s, rp_r)

    def put_rows(src, value, dst, send, recv):
        for i in range(16):
            src[i] = value[i : i + 1, :]
        for i in range(16):
            own = jnp.logical_and(is_self == 1, row_slot == i)

            @pl.when(own)
            def _(i=i):
                dst[i] = src[i]

            @pl.when(jnp.logical_not(own))
            def _(i=i):
                remote(src.at[i], dst.at[row_slot], send.at[i], recv.at[row_slot], row_dev(i)).start()

    def get_rows(src, dst, send, recv):
        for i in range(16):
            own = jnp.logical_and(is_self == 1, row_slot == i)

            @pl.when(jnp.logical_not(own))
            def _(i=i):
                remote(src.at[i], dst.at[i], send.at[i], recv.at[i], row_dev(i)).wait()

        return jnp.concatenate([dst[i] for i in range(16)], axis=0)

    put_rows(gas, scattered(gap, rsg, rg_s, rg_r), gad, ga_s, ga_r)
    pre = scattered(prep, rsp, rp_s, rp_r)
    put_rows(acs, (pre * sigmoid(pre)).astype(BF).astype(F32), acd, aa_s, aa_r)
    pre_slope = slope(pre)

    gpf[t] = (get_rows(gas, gad, ga_s, ga_r) * pre_slope).astype(BF)
    for d in range(1, NT):
        start(remote(gpf.at[t], gpf.at[t], gp_s.at[d], gp_r.at[t], tdev(d)))
    acf[t] = get_rows(acs, acd, aa_s, aa_r).astype(BF)
    for d in range(1, NT):
        start(remote(acf.at[t], acf.at[t], af_s.at[d], af_r.at[t], tdev(d)))

    wait_slots(gpf, gp_s, gp_r)
    grads = gpf[...].reshape(128, 640)
    gpt[...] = mm(grads[:, 0:512], sall[:, :, :, 0:1152].reshape(512, 1152)) + mm(grads[:, 512:640], srest[...])
    ges[...] = gpt[other, 512:1152].astype(BF)
    start(remote(ges, ger, ge_sem.at[0], ge_sem.at[1], sibling))
    gos[0] = (gpt[0:64, 0:640] * mask0).astype(BF)
    gos[1] = (gpt[64:128, 0:640] * mask1).astype(BF)
    start(remote(gos.at[0], gor.at[k], go_s.at[0], go_r.at[k], chip(m - 1, 1)))

    @pl.when(k == 1)
    def _():
        remote(gos.at[1], gor.at[1], go_s.at[1], go_r.at[1], sibling).start()

    @pl.when(k == 0)
    def _():
        gor[0] = gos[1]

    wait_slots(acf, af_s, af_r)
    acts = acf[...].reshape(128, 640)
    part = mm(acts[:, 0:512], rall[:, :, :, 0:1024].reshape(512, 1024)) + mm(acts[:, 512:640], rrest[...])
    low, high = part[0:64], part[64:128]
    kf = k.astype(F32)
    tks[...] = (low * kf + high * (1.0 - kf)).astype(BF)
    start(remote(tks, tkr, tk_sem.at[0], tk_sem.at[1], sibling))
    own_tokens = low * (1.0 - kf) + high * kf

    remote(ges, ger, ge_sem.at[0], ge_sem.at[1], sibling).wait_recv()
    remote(gos.at[0], gor.at[1], go_s.at[0], go_r.at[1], sibling).wait_recv()

    @pl.when(k == 1)
    def _():
        remote(gos.at[0], gor.at[0], go_s.at[0], go_r.at[0], sibling).wait_recv()

    mine = pl.ds(pl.multiple_of(64 * k, 64), 64)
    even = gpt[mine, 512:1152] + ger[...].astype(F32)
    odd = gor[0].astype(F32) + gor[1].astype(F32)
    ungather = select(patch_place(iota((256, 256), 1)) == iota((256, 256), 0))
    narrow = iota((64, 128), 1) < 16
    for f in range(2):
        if f == 0:
            tile, mains, base = even[:, 0:128], even[:, 128:640], 4
        else:
            tile, mains, base = odd[:, 512:640], odd[:, 0:512], 0
        main = jnp.concatenate([mains[:, 128 * s : 128 * s + 128] for s in range(4)], axis=0)
        tails = []
        for s in range(4):
            by = (128 - 16 * (s + base)) % 128
            tails.append(jnp.where(narrow, tile if by == 0 else pltpu.roll(tile, by, 1), 0.0))
        taps = jnp.concatenate([main, jnp.concatenate(tails, axis=0)], axis=1)
        top = taps.astype(BF)
        bottom = (taps - top.astype(F32)).astype(BF)
        grad = (mm(ungather, top) + mm(ungather, bottom)) * bm[...]
        gh[f] = grad
        pbuf[f : f + 1, :] = jnp.sum(grad * ac[f], axis=0, keepdims=True)

    inner = pbuf[...] * excite * (1.0 - excite)
    psl2[t] = exact(mmt, inner, sqoe[...])
    for d in range(1, NT):
        start(remote(psl2.at[t], psl2.at[t], pq_s.at[d], pq_r.at[t], tdev(d)))

    remote(tks, tkr, tk_sem.at[0], tk_sem.at[1], sibling).wait_recv()
    llm[...] = ((own_tokens + tkr[...].astype(F32)) * live(ctx)).astype(BF)

    wait_slots(psl2, pq_s, pq_r)
    grad_squeezed = jnp.sum(psl2[...], axis=0) * slope(squeezed)
    grad_pooled = exact(mmt, grad_squeezed, sqie[...]) * (1.0 / 196.0)
    outof = select(padded_place(iota((196, 256), 0)) == iota((196, 256), 1))
    for f in range(2):
        grad_active = gh[f] * excite[f : f + 1, :] + grad_pooled[f : f + 1, :]
        put_shifts(f, grad_active * sl[f])
        total = gh[f]
        for dy in range(3):
            for dx in range(3):
                total = total + mmt(xs[f, 2 - dx, 16 * (2 - dy) : 16 * (2 - dy) + 256, :], wc[3 * dy + dx])
        gout[f] = mm(outof, total.astype(BF))[:, 0:144].astype(BF)

    for copy in sent:
        copy.wait_send()
    remote(obuf, p0.at[0:64], o_s.at[0], o_r.at[0], sibling).wait_send()

    @pl.when(k == 1)
    def _():
        remote(obuf, p0.at[0:64], o_s.at[1], o_r.at[0], sibling).wait_send()
        remote(gos.at[1], gor.at[1], go_s.at[1], go_r.at[1], sibling).wait_send()


def per_device(features, group_kernel, squeeze_in, squeeze_out, sampler_kernel, readout_kernel, frame_clip, clip_keep, token_cotangent):
    V = pltpu.VMEM
    dma = pltpu.SemaphoreType.DMA
    scratch = [
        V((NZ, NX, 16, 1408), BF),
        V((NZ, NX, 16, 1152), BF),
        V((128, 1152), BF),
        V((128, 1024), BF),
        V((512, 128), F32),
        V((512, 128), F32),
        V((2, 64, 1024), BF),
        V((9, 256, 256), BF),
        V((2, 3, 288, 256), BF),
        V((2, 256, 256), F32),
        V((2, 256, 256), F32),
        V((2, 256, 256), F32),
        V((256, 256), F32),
        V((2, 256, 256), F32),
        V((256, 288), BF),
        V((288, 256), BF),
        V((8, 256), F32),
        V((NT, 8, 288), F32),
        V((NT, 8, 288), F32),
        V((128, 640), BF),
        V((128, 640), BF),
        V((64, 640), BF),
        V((8, 16, 640), BF),
        V((8, 16, 640), BF),
        V((8, 16, 640), BF),
        V((8, 16, 640), BF),
        V((16, 1, 640), F32),
        V((16, 1, 640), F32),
        V((16, 1, 640), F32),
        V((16, 1, 640), F32),
        V((8, 16, 640), BF),
        V((8, 16, 640), BF),
        V((128, 1152), F32),
        V((64, 640), BF),
        V((64, 640), BF),
        V((2, 64, 640), BF),
        V((2, 64, 640), BF),
        V((64, 1024), BF),
        V((64, 1024), BF),
        dma((2,)),
        dma((4,)), dma((4,)),
        dma((9,)), dma((8,)), dma((2,)),
        dma((8,)), dma((8,)),
        dma((4,)), dma((2,)), dma((2,)),
        dma((8,)), dma((8,)),
        dma((8,)), dma((8,)),
        dma((2,)),
        dma((2,)), dma((2,)),
        dma((8,)), dma((8,)),
        dma((8,)), dma((8,)),
        dma((16,)), dma((16,)),
        dma((16,)), dma((16,)),
        dma((8,)), dma((8,)),
        dma((8,)), dma((8,)),
        dma((2,)),
        dma((2,)), dma((2,)),
        dma((2,)),
    ]
    spec = pl.BlockSpec(memory_space=pltpu.VMEM)
    return pl.pallas_call(
        kernel,
        out_shape=(jax.ShapeDtypeStruct((64, 1024), BF), jax.ShapeDtypeStruct((2, 196, 144), BF)),
        in_specs=[spec] * 9,
        out_specs=(spec, spec),
        scratch_shapes=scratch,
        compiler_params=pltpu.CompilerParams(
            collective_id=0, has_side_effects=True, vmem_limit_bytes=48 * 1024 * 1024
        ),
        cost_estimate=pl.CostEstimate(flops=3_000_000_000, bytes_accessed=1_000_000, transcendentals=1_000_000),
        name="connector",
    )(
        features,
        group_kernel,
        squeeze_in,
        squeeze_out,
        sampler_kernel.reshape(144, 144),
        readout_kernel,
        frame_clip.reshape(1, 128),
        clip_keep.reshape(1, 16),
        token_cotangent,
    )


def solution(mesh):
    placed = (
        P("ctx", None, "tp"),
        P(None, "tp", None),
        P("tp", None),
        P(None, "tp"),
        P("ctx", None, "tp"),
        P("ctx", "tp"),
        P(),
        P(),
        P("ctx", "tp"),
    )
    return jax.shard_map(
        per_device,
        mesh=mesh,
        in_specs=placed,
        out_specs=(P("ctx", "tp"), P("ctx", None, "tp")),
        check_vma=False,
    )
```

```python
import jax
import jax.numpy as jnp
from jax import lax
from jax.experimental import pallas as pl
from jax.experimental.pallas import tpu as pltpu
from jax.sharding import PartitionSpec as P

NX, NZ, NT = 4, 8, 8
BF = jnp.bfloat16
F32 = jnp.float32
MESH = pl.DeviceIdType.MESH
SLOT = (0, 128, 256, 384, 640, 768, 896, 1024)


def iota(shape, dim):
    return lax.broadcasted_iota(jnp.int32, shape, dim)


def select(hit):
    return jnp.where(hit, 1.0, 0.0).astype(BF)


def mm(a, b):
    return jnp.dot(a, b, preferred_element_type=F32)


def mmt(a, b):
    return lax.dot_general(a, b, (((1,), (1,)), ((), ())), preferred_element_type=F32)


def exact(dot, value, weight):
    high = value.astype(BF)
    left = value - high.astype(F32)
    middle = left.astype(BF)
    low = (left - middle.astype(F32)).astype(BF)
    return dot(high, weight) + (dot(middle, weight) + dot(low, weight))


def sigmoid(v):
    return jax.nn.sigmoid(v)


def slope(v):
    s = sigmoid(v)
    return s * (1.0 + v * (1.0 - s))


def padded_place(cell):
    row = (cell * 4682) >> 16
    return (row + 1) * 16 + (cell - 14 * row) + 1


def token_at(row):
    return 4 * (row & 15) + 2 * ((row >> 4) & 1) + ((row >> 5) & 1)


def patch_place(r):
    s = r >> 6
    token = token_at(r & 63)
    a = token >> 3
    b = token & 7
    return (2 * a + (s >> 1)) * 16 + 2 * b + (s & 1)


def third(v):
    return (v >= 48).astype(jnp.int32) + (v >= 96).astype(jnp.int32)


def kernel(
    feat_h, gk_h, sqi_h, sqo_h, samp_h, read_h, fclip, keep, cot_h,
    llm, gout,
    feat, gk, samp, read,
    sall, rall, srest, rrest, fta, ftb, cotb, wc, xs, cv, ac, sl, bm, gh, sqie, sqoe, pbuf, psl, psl2,
    p0, p1, obuf, prep, rsp, gap, rsg, gas, gad, acs, acd, gpf, acf, gpt, ges, ger, gos, gor, tks, tkr,
    load, cot_sem, s_out, s_in, r_out, r_in, pair, e_sem, o_s, o_r, ge_sem, go_s, go_r, tk_sem,
):
    ctx = lax.axis_index("ctx")
    t = lax.axis_index("tp")
    k = lax.rem(ctx, 2)
    m = lax.div(ctx, 2)
    z = lax.rem(m, NZ)
    x = lax.div(m, NZ)
    chips = NX * NZ

    def dev(xx, zz, kk, tt):
        return ((xx * NZ + zz) * 2 + kk, tt)

    def chip(mm_, kk):
        return (lax.rem(mm_ + chips, chips) * 2 + kk, t)

    def zdev(d):
        return dev(x, lax.rem(z + d + NZ, NZ), k, t)

    def xdev(d):
        return dev(lax.rem(x + d + NX, NX), z, k, t)

    def tdev(d):
        return (ctx, lax.rem(t + d, NT))

    sibling = (m * 2 + (1 - k), t)
    twist = lax.rem(m + lax.div(t, 4), 2)
    row_slot = lax.div(m, 2)
    is_self = (t < 4).astype(jnp.int32)

    def frame_chunk(o):
        return 4 * lax.rem(o, 2) + 2 * lax.rem(lax.div(o, 2), 2) + lax.rem(lax.div(o, 4) + m, 2)

    def decoder_chunk(o):
        return 4 * lax.rem(lax.div(o, 2), 2) + 2 * lax.rem(o, 2) + lax.rem(lax.div(o, 4) + m, 2)

    def row_dev(i):
        return ((2 * i + twist) * 2 + k, t)

    def remote(src, dst, send, recv, where):
        return pltpu.make_async_remote_copy(
            src_ref=src, dst_ref=dst, send_sem=send, recv_sem=recv, device_id=where, device_id_type=MESH
        )

    def exchange(source, slots, slot, which):
        for d in range(1, NT):
            o = lax.rem(t + d, NT)
            remote(source(o), slots.at[slot], pair.at[which, 0], pair.at[which, 1], tdev(d)).start()
        all_of = remote(slots.at[0 : NT - 1], slots.at[0 : NT - 1], pair.at[which, 0], pair.at[which, 1], tdev(1))
        leaving.append(all_of.wait_send)
        return all_of.wait_recv

    leaving = []
    coming = {}

    def start(copy):
        copy.start()
        leaving.append(copy.wait_send)

    def arrive(*names):
        for name in names:
            coming.pop(name)()

    def finish():
        arrive(*list(coming))
        for left in leaving:
            left()

    barrier = pltpu.get_barrier_semaphore()

    def hello(where):
        pl.semaphore_signal(barrier, inc=1, device_id=where, device_id_type=MESH)

    local = []
    for i, (src, dst) in enumerate(
        (
            (read_h, read), (samp_h, samp), (feat_h, feat), (gk_h, gk), (cot_h, cotb.at[k]),
            (sqi_h, sqie.at[0:144]), (sqo_h, sqoe.at[0:144]),
        )
    ):
        local.append(pltpu.make_async_copy(src, dst, load.at[i]))
        local[-1].start()

    hello(sibling)
    for d in range(1, NX):
        hello(xdev(d))
    hello(zdev(1))
    hello(zdev(-1))
    for d in range(1, NT):
        hello(tdev(d))
    hello(chip(m - 1, 1))

    @pl.when(k == 1)
    def _():
        hello(chip(m + 1, 0))
        hello(chip(m + 1, 1))

    trade = [lax.rem(row_slot + j, 16) for j in range(16)]

    @pl.when(is_self == 0)
    def _():
        hello(row_dev(trade[0]))

    for j in range(1, 16):
        hello(row_dev(trade[j]))

    own = 4 * z + x
    local[0].wait()
    rall[own, :, 0:1024] = read[0:16, :]
    last = read[16:18, :].astype(F32)
    for j in range(2):
        for p in range(8):
            fta[256 + j * 8 + p : 257 + j * 8 + p, :] = last[j : j + 1, 128 * p : 128 * p + 128]
    rall[own, :, 1024:1152] = fta[256:272, :].astype(BF)
    local[1].wait()
    ftb[0:144, :] = jnp.zeros((144, 128), F32)
    fta[0:144, :] = samp[:, 0:128].astype(F32)
    ftb[0:144, 0:16] = samp[:, 128:144].astype(F32)
    rest = jnp.zeros((16, 128), F32)
    for s in range(8):
        sall[own, :, SLOT[s] : SLOT[s] + 128] = fta[pl.ds(s, 16, stride=8), :].astype(BF)
        tail = ftb[pl.ds(s, 16, stride=8), :]
        rest = rest + (tail if s == 0 else pltpu.roll(tail, 16 * s, 1))
    sall[own, :, 512:640] = rest.astype(BF)
    sall[own, :, 1152:1280] = fta[128:144, :].astype(BF)
    sall[own, :, 1280:1408] = ftb[128:144, :].astype(BF)

    pl.semaphore_wait(barrier, 1 + (NX - 1) + 2 + (NT - 1) + (1 + 2 * k) + 16 - is_self)

    def zi(d):
        return lax.rem(z + d + NZ, NZ)

    def xi(e):
        return lax.rem(x + e, NX)

    def hop(d):
        return {-1: 0, -2: 1, -3: 2, 1: 3, 2: 4, 3: 5, 4: 6}[d]

    class Gather:
        def __init__(self, ref, out, into, way):
            self.ref, self.out, self.into, self.way = ref, out, into, way

        def block(self, d, e):
            return self.ref.at[4 * zi(d) + xi(e)]

        def send(self, d, e, sem, where):
            remote(self.block(d, e), self.block(d, e), self.out.at[0], self.into.at[sem], where).start()

        def got(self, d, e, sem):
            remote(self.block(d, e), self.block(d, e), self.out.at[0], self.into.at[sem], sibling).wait_recv()

        def a_z(self, e):
            if e:
                self.got(0, e, e)
            self.send(0, e, 4 + 7 * e + hop(-1), zdev(1))
            self.send(0, e, 4 + 7 * e + hop(1), zdev(-1))

        def a_start(self):
            for e in (1, 3, 2):
                self.send(0, 0, (-e) % 4, xdev(e))
            self.a_z(0)

        def a_ring(self, i, *columns):
            for e in columns:
                at = 4 + 7 * e
                self.got(-i, e, at + hop(-i))
                self.got(i, e, at + hop(i))
                if i < 3:
                    self.send(-i, e, at + hop(-i - 1), zdev(1))
                    self.send(i, e, at + hop(i + 1), zdev(-1))
                else:
                    way = 1 if e % 2 == 0 else -1
                    self.send(-3 * way, e, at + hop(4), zdev(way))

        def a_end(self):
            for e in (0, 1, 3, 2):
                self.got(4, e, 4 + 7 * e + hop(4))

        def b_at(self, d, e):
            return 7 + 3 * (d % 8) + e - 1

        def b_x(self, d):
            self.send(d, 0, self.b_at(d, 3), xdev(1))
            self.send(d, 0, self.b_at(d, 1), xdev(-1))

        def b_start(self):
            self.send(0, 0, hop(-1), zdev(1))
            self.send(0, 0, hop(1), zdev(-1))
            self.b_x(0)

        def b_ring(self, i):
            if i == 4:
                self.got(4, 0, hop(4))
                self.b_x(4)
                return
            self.got(-i, 0, hop(-i))
            self.got(i, 0, hop(i))
            if i < 3:
                self.send(-i, 0, hop(-i - 1), zdev(1))
                self.send(i, 0, hop(i + 1), zdev(-1))
            else:
                self.send(-3 * self.way, 0, hop(4), zdev(self.way))
            self.b_x(-i)
            self.b_x(i)

        def b_pass(self, *rows):
            for d in rows:
                e = 3 if d % 2 == 0 else 1
                self.got(d, e, self.b_at(d, e))
                self.send(d, e, self.b_at(d, 2), xdev(1 if e == 3 else -1))

        def b_end(self):
            for d in (0, 1, -1, 2, -2, 3, -3, 4):
                e = 1 if d % 2 == 0 else 3
                self.got(d, e, self.b_at(d, e))
            for d in (0, 1, -1, 2, -2, 3, -3, 4):
                self.got(d, 2, self.b_at(d, 2))

        def end(self):
            cores(self.a_end, self.b_end)

    def cores(zero, one):
        pl.when(k == 0)(lambda: zero() and None)
        pl.when(k == 1)(lambda: one() and None)

    R = Gather(rall, r_out, r_in, 1)
    S = Gather(sall, s_out, s_in, -1)

    def weights_sent():
        remote(rall.at[0:31], rall.at[0:31], r_out.at[0], r_out.at[0], sibling).wait_send()
        remote(sall.at[0:31], sall.at[0:31], s_out.at[0], s_out.at[0], sibling).wait_send()

    leaving.append(weights_sent)

    def pump(n):
        cores(
            [
                lambda: (R.a_start(), S.a_start()),
                lambda: (R.a_z(1), R.a_z(3)),
                lambda: (R.a_z(2), R.a_ring(1, 0)),
                lambda: R.a_ring(1, 1, 3),
                lambda: (R.a_ring(1, 2), R.a_ring(2, 0), S.a_z(1), S.a_z(3)),
                lambda: R.a_ring(2, 1, 3),
                lambda: (R.a_ring(2, 2), R.a_ring(3, 0), S.a_z(2)),
                lambda: (R.a_ring(3, 1, 3, 2), S.a_ring(1, 0)),
                lambda: S.a_ring(1, 1, 3, 2),
                lambda: S.a_ring(2, 0, 1),
                lambda: S.a_ring(2, 3, 2),
                lambda: S.a_ring(3, 0, 1),
                lambda: S.a_ring(3, 3, 2),
            ][n],
            [
                lambda: (R.b_start(), S.b_start()),
                lambda: R.b_ring(1),
                lambda: (R.b_ring(2), R.b_pass(0)),
                lambda: (R.b_ring(3), S.b_ring(1)),
                lambda: (R.b_ring(4), R.b_pass(1, -1)),
                lambda: (R.b_pass(2, -2), S.b_ring(2)),
                lambda: (R.b_pass(3, -3, 4), S.b_ring(3), S.b_pass(0)),
                lambda: S.b_ring(4),
                lambda: S.b_pass(1, -1),
                lambda: S.b_pass(2, -2),
                lambda: S.b_pass(3, -3),
                lambda: S.b_pass(4),
                lambda: None,
            ][n],
        )

    pump(0)
    start(remote(cot_h, cotb.at[k], cot_sem.at[0], cot_sem.at[1], sibling))
    coming["cot"] = remote(cot_h, cotb.at[1 - k], cot_sem.at[0], cot_sem.at[1], sibling).wait_recv
    cell = iota((256, 256), 0)
    cy, cx = cell >> 4, cell & 15
    inside = jnp.logical_and(
        jnp.logical_and(cy >= 1, cy <= 14), jnp.logical_and(cx >= 1, cx <= 14)
    )
    bm[...] = jnp.where(inside, 1.0, 0.0)
    into = select(padded_place(iota((256, 196), 1)) == iota((256, 196), 0))
    channel = iota((144, 48), 0)
    spread = select(channel - 48 * third(channel) == iota((144, 48), 1))
    same_group = third(iota((144, 144), 0)) == third(iota((144, 144), 1))
    blank = jnp.zeros((112, 196), BF)

    def centre(f):
        if f == 0:
            local[2].wait()
        return mmt(into, jnp.concatenate([feat[f], blank], axis=0))

    def put_shifts(f, value):
        xs[0, f, 16:272, :] = pltpu.roll(value, 1, 0).astype(BF)
        xs[1, f, 16:272, :] = value.astype(BF)
        xs[2, f, 16:272, :] = pltpu.roll(value, 255, 0).astype(BF)

    for f in range(2):
        for j in range(3):
            xs[j, f, 0:16, :] = jnp.zeros((16, 256), BF)
            xs[j, f, 272:288, :] = jnp.zeros((16, 256), BF)
        put_shifts(f, centre(f))
        pump(1 + f)
    local[3].wait()
    for tap in range(9):
        wc[tap] = jnp.zeros((256, 256), BF)
        dense = jnp.where(same_group, mm(spread, gk[tap]), 0.0)
        wc[tap, 0:144, 0:144] = dense.astype(BF)
        if tap == 4:
            pump(3)
    sqoe[144:256, :] = jnp.zeros((112, 288), BF)
    sqie[144:256, :] = jnp.zeros((112, 288), BF)
    pbuf[...] = jnp.zeros((8, 256), F32)
    pump(4)

    both = jnp.zeros((512, 256), F32)
    for dy in range(3):
        for dx in range(3):
            window = xs[dx, :, 16 * dy : 16 * dy + 256, :].reshape(512, 256)
            both = both + mmt(window, wc[3 * dy + dx])
        pump(5 + dy)
    for f in range(2):
        total = both[256 * f : 256 * f + 256]
        cv[f] = total
        act = total * sigmoid(total) * bm[...]
        ac[f] = act
        pbuf[f : f + 1, :] = jnp.sum(act, axis=0, keepdims=True) * (1.0 / 196.0)
    local[5].wait()
    local[6].wait()

    def put_sums(slots, sums, which):
        slots[t] = jnp.zeros((1, 768), F32)
        slots[t, :, 0:288] = sums[0:1]
        slots[t, :, 384:672] = sums[1:2]
        return exchange(lambda o: slots.at[t], slots, t, which)

    def get_sums(slots):
        both_rows = jnp.sum(slots[...], axis=0)
        return jnp.concatenate([both_rows[:, 0:288], both_rows[:, 384:672], jnp.zeros((6, 288), F32)], axis=0)

    coming["ps"] = put_sums(psl, exact(mm, pbuf[...], sqie[...]), 0)
    pump(8)

    clips = fclip[...].astype(F32)
    lane = iota((64, 128), 1)
    clip_col = jnp.sum(jnp.where(lane == 2 * token_at(iota((64, 128), 0)), clips, 0.0), axis=1, keepdims=True)
    before = jnp.logical_and((lane & 1) == 0, clips < clip_col)
    first = jnp.sum(jnp.where(before, 1.0, 0.0), axis=1, keepdims=True)
    lane16 = iota((64, 16), 1).astype(F32)
    kept = jnp.sum(jnp.where(lane16 == clip_col, keep[...].astype(F32), 0.0), axis=1, keepdims=True)
    place = (token_at(iota((64, 1), 0)).astype(F32) - first) * 64.0

    def live(d):
        return jnp.where(place + jnp.asarray(d, jnp.int32).astype(F32) < kept, 1.0, 0.0)

    lane1 = iota((1, 128), 1)

    def pair_mask(c):
        now = jnp.sum(jnp.where(lane1 == 2 * c, clips, 0.0), axis=1, keepdims=True)
        was = jnp.sum(jnp.where(lane1 == 2 * c - 1, clips, 0.0), axis=1, keepdims=True)
        return jnp.where(jnp.logical_and(now == was, iota((1, 1), 0) + c > 0), 1.0, 0.0)

    mask0, mask1 = pair_mask(2 * m), pair_mask(2 * m + 1)

    for f in range(2):
        sl[f] = slope(cv[f]) * bm[...]
        pump(9 + f)

    arrive("ps")
    squeezed = get_sums(psl)
    excite = sigmoid(exact(mmt, squeezed * sigmoid(squeezed), sqoe[...]))
    other = pl.ds(pl.multiple_of(64 * (1 - k), 64), 64)
    gather = select(patch_place(iota((256, 256), 0)) == iota((256, 256), 1))
    for f in range(2):
        hidden = xs[1, f, 16:272, :].astype(F32) + ac[f] * excite[f : f + 1, :]
        taps = mm(gather, hidden.astype(BF))
        base = 4 * (1 - f)
        rest = jnp.zeros((64, 128), F32)
        for s in range(4):
            tail = taps[64 * s : 64 * s + 64, 128:256]
            by = 16 * (s + base)
            rest = rest + (tail if by == 0 else pltpu.roll(tail, by, 1))
        main = taps[:, 0:128].astype(BF)
        if f == 0:
            mine = pl.ds(pl.multiple_of(64 * k, 64), 64)
            p1[mine, 0:128] = rest.astype(BF)
            for s in range(4):
                p1[mine, 128 * (s + 1) : 128 * (s + 2)] = main[64 * s : 64 * s + 64]
            start(remote(p1.at[mine], p1.at[mine], e_sem.at[0], e_sem.at[1], sibling))
            coming["even"] = lambda: remote(p1.at[other], p1.at[other], e_sem.at[0], e_sem.at[1], sibling).wait_recv()
        else:
            obuf[:, 512:640] = rest.astype(BF)
            for s in range(4):
                obuf[:, 128 * s : 128 * (s + 1)] = main[64 * s : 64 * s + 64]

    def send_odd():
        @pl.when(k == 0)
        def _():
            p0[64:128, :] = obuf[...]
            remote(obuf, p0.at[64:128], o_s.at[0], o_r.at[1], sibling).start()

        @pl.when(k == 1)
        def _():
            remote(obuf, p0.at[0:64], o_s.at[0], o_r.at[0], chip(m + 1, 1)).start()
            remote(obuf, p0.at[0:64], o_s.at[1], o_r.at[0], chip(m + 1, 0)).start()

    def odd_sent():
        remote(obuf, p0.at[0:64], o_s.at[0], o_r.at[0], sibling).wait_send()

        @pl.when(k == 1)
        def _():
            remote(obuf, p0.at[0:64], o_s.at[1], o_r.at[0], sibling).wait_send()

    def odd_here():
        remote(obuf, p0.at[0:64], o_s.at[0], o_r.at[0], sibling).wait_recv()

        @pl.when(k == 1)
        def _():
            remote(obuf, p0.at[64:128], o_s.at[0], o_r.at[1], sibling).wait_recv()

    send_odd()
    leaving.append(odd_sent)
    coming["odd"] = odd_here

    local[4].wait()
    R.end()
    fta[...] = rall[:, :, 1024:1152].reshape(512, 128).astype(F32)
    for p in range(8):
        rrest[0:64, 128 * p : 128 * p + 128] = fta[pl.ds(p, 64, stride=8), :].astype(BF)
    rrest[64:128, :] = jnp.zeros((64, 1024), BF)
    arrive("cot")
    order = select(token_at(iota((64, 64), 0)) == iota((64, 64), 1))
    back = jnp.concatenate([mm(order, cotb[0]).astype(BF), mm(order, cotb[1]).astype(BF)], axis=0)
    alive = jnp.concatenate([live(2 * m), live(2 * m + 1)], axis=0)
    gap[:, :, 0:512] = (
        (mmt(back, rall[:, :, 0:1024].reshape(512, 1024)) * alive).astype(BF).reshape(8, 16, 512)
    )
    pump(11)
    gap[:, :, 512:640] = (mmt(back, rrest[...]) * alive).astype(BF).reshape(8, 16, 128)

    def scattered(parts, chunk, slots):
        total = parts[chunk].astype(F32)
        for d in range(1, NT):
            total = total + slots[lax.rem(t + d, NT)].astype(F32)
        return total

    coming["rg"] = exchange(lambda o: gap.at[decoder_chunk(o)], rsg, t, 1)
    pump(12)

    def put_rows(src, value, dst, which):
        for i in range(16):
            src[i] = value[i : i + 1, :]

        @pl.when(is_self == 1)
        def _():
            dst[row_slot] = src[row_slot]

        @pl.when(is_self == 0)
        def _():
            i = trade[0]
            remote(src.at[i], dst.at[row_slot], pair.at[which, 0], pair.at[which, 1], row_dev(i)).start()

        for i in trade[1:]:
            remote(src.at[i], dst.at[row_slot], pair.at[which, 0], pair.at[which, 1], row_dev(i)).start()

        def both(wait):
            @pl.when(is_self == 1)
            def _():
                wait(remote(src.at[0:15], dst.at[0:15], pair.at[which, 0], pair.at[which, 1], sibling))

            @pl.when(is_self == 0)
            def _():
                wait(remote(src, dst, pair.at[which, 0], pair.at[which, 1], sibling))

        leaving.append(lambda: both(lambda copy: copy.wait_send()))
        return lambda: both(lambda copy: copy.wait_recv())

    def get_rows(dst):
        return jnp.concatenate([dst[i] for i in range(16)], axis=0)

    arrive("rg")
    coming["ga"] = put_rows(gas, scattered(gap, decoder_chunk(t), rsg), gad, 3)
    arrive("even", "odd")
    S.end()
    fta[...] = sall[:, :, 1152:1280].reshape(512, 128).astype(F32)
    ftb[...] = sall[:, :, 1280:1408].reshape(512, 128).astype(F32)
    rest = jnp.zeros((64, 128), F32)
    for s in range(8):
        srest[0:64, SLOT[s] : SLOT[s] + 128] = fta[pl.ds(s, 64, stride=8), :].astype(BF)
        tail = ftb[pl.ds(s, 64, stride=8), :]
        rest = rest + (tail if s == 0 else pltpu.roll(tail, 16 * s, 1))
    srest[0:64, 512:640] = rest.astype(BF)
    srest[64:128, :] = jnp.zeros((64, 1152), BF)

    mask_col = jnp.concatenate(
        [jnp.broadcast_to(mask0, (64, 1)), jnp.broadcast_to(mask1, (64, 1))], axis=0
    )

    def pre_part(w0, w1):
        return mmt(p0[...], w0) * mask_col + mmt(p1[...], w1)

    prep[:, :, 0:512] = (
        pre_part(sall[:, :, 0:640].reshape(512, 640), sall[:, :, 512:1152].reshape(512, 640))
        .astype(BF)
        .reshape(8, 16, 512)
    )
    prep[:, :, 512:640] = pre_part(srest[:, 0:640], srest[:, 512:1152]).astype(BF).reshape(8, 16, 128)
    coming["rp"] = exchange(lambda o: prep.at[frame_chunk(o)], rsp, t, 2)

    arrive("rp")
    pre = scattered(prep, frame_chunk(t), rsp)
    pre_slope = slope(pre)
    arrive("ga")
    in_frames = frame_chunk(t)
    gpf[in_frames] = (get_rows(gad) * pre_slope).astype(BF)
    coming["gp"] = exchange(lambda o: gpf.at[in_frames], gpf, in_frames, 5)
    coming["aa"] = put_rows(acs, (pre * sigmoid(pre)).astype(BF).astype(F32), acd, 4)
    arrive("gp")
    grads = gpf[...].reshape(128, 640)
    gpt[...] = mm(grads[:, 0:512], sall[:, :, 0:1152].reshape(512, 1152)) + mm(grads[:, 512:640], srest[...])
    ges[...] = gpt[other, 512:1152].astype(BF)
    start(remote(ges, ger, ge_sem.at[0], ge_sem.at[1], sibling))
    coming["ge"] = remote(ges, ger, ge_sem.at[0], ge_sem.at[1], sibling).wait_recv
    gos[0] = (gpt[0:64, 0:640] * mask0).astype(BF)
    gos[1] = (gpt[64:128, 0:640] * mask1).astype(BF)
    start(remote(gos.at[0], gor.at[k], go_s.at[0], go_r.at[k], chip(m - 1, 1)))

    @pl.when(k == 1)
    def _():
        remote(gos.at[1], gor.at[1], go_s.at[1], go_r.at[1], sibling).start()

    @pl.when(k == 0)
    def _():
        gor[0] = gos[1]

    def grad_odd_sent():
        @pl.when(k == 1)
        def _():
            remote(gos.at[1], gor.at[1], go_s.at[1], go_r.at[1], sibling).wait_send()

    def grad_odd_here():
        remote(gos.at[0], gor.at[1], go_s.at[0], go_r.at[1], sibling).wait_recv()

        @pl.when(k == 1)
        def _():
            remote(gos.at[0], gor.at[0], go_s.at[0], go_r.at[0], sibling).wait_recv()

    leaving.append(grad_odd_sent)
    coming["go"] = grad_odd_here

    arrive("aa")
    in_decoder = decoder_chunk(t)
    acf[in_decoder] = get_rows(acd).astype(BF)
    coming["af"] = exchange(lambda o: acf.at[in_decoder], acf, in_decoder, 6)

    arrive("ge", "go")
    mine = pl.ds(pl.multiple_of(64 * k, 64), 64)
    even = gpt[mine, 512:1152] + ger[...].astype(F32)
    odd = gor[0].astype(F32) + gor[1].astype(F32)
    ungather = select(patch_place(iota((256, 256), 1)) == iota((256, 256), 0))
    narrow = iota((64, 128), 1) < 16
    for f in range(2):
        if f == 0:
            tile, mains, base = even[:, 0:128], even[:, 128:640], 4
        else:
            tile, mains, base = odd[:, 512:640], odd[:, 0:512], 0
        main = jnp.concatenate([mains[:, 128 * s : 128 * s + 128] for s in range(4)], axis=0)
        tails = []
        for s in range(4):
            by = (128 - 16 * (s + base)) % 128
            tails.append(jnp.where(narrow, tile if by == 0 else pltpu.roll(tile, by, 1), 0.0))
        taps = jnp.concatenate([main, jnp.concatenate(tails, axis=0)], axis=1)
        top = taps.astype(BF)
        bottom = (taps - top.astype(F32)).astype(BF)
        grad = (mm(ungather, top) + mm(ungather, bottom)) * bm[...]
        gh[f] = grad
        pbuf[f : f + 1, :] = jnp.sum(grad * ac[f], axis=0, keepdims=True)

    inner = pbuf[...] * excite * (1.0 - excite)
    coming["pq"] = put_sums(psl2, exact(mm, inner, sqoe[...]), 7)
    arrive("af")
    acts = acf[...].reshape(128, 640)
    part = mm(acts[:, 0:512], rall[:, :, 0:1024].reshape(512, 1024)) + mm(acts[:, 512:640], rrest[...])
    low, high = part[0:64], part[64:128]
    kf = k.astype(F32)
    tks[...] = (low * kf + high * (1.0 - kf)).astype(BF)
    start(remote(tks, tkr, tk_sem.at[0], tk_sem.at[1], sibling))
    own_tokens = low * (1.0 - kf) + high * kf
    coming["tk"] = remote(tks, tkr, tk_sem.at[0], tk_sem.at[1], sibling).wait_recv

    arrive("pq")
    grad_squeezed = get_sums(psl2) * slope(squeezed)
    grad_pooled = exact(mmt, grad_squeezed, sqie[...]) * (1.0 / 196.0)
    outof = select(padded_place(iota((196, 256), 0)) == iota((196, 256), 1))
    for f in range(2):
        grad_active = gh[f] * excite[f : f + 1, :] + grad_pooled[f : f + 1, :]
        put_shifts(f, grad_active * sl[f])
    both = gh[...].reshape(512, 256)
    for dy in range(3):
        for dx in range(3):
            window = xs[2 - dx, :, 16 * (2 - dy) : 16 * (2 - dy) + 256, :].reshape(512, 256)
            both = both + mm(window, wc[3 * dy + dx])
    for f in range(2):
        turned = both[256 * f : 256 * f + 256].T[0:144].astype(BF)
        gout[f] = mmt(turned, outof).astype(BF)

    arrive("tk")
    rows = ((own_tokens + tkr[...].astype(F32)) * live(ctx)).astype(BF)
    llm[...] = mm(select(token_at(iota((64, 64), 1)) == iota((64, 64), 0)), rows).astype(BF)
    finish()


def per_device(features, group_kernel, squeeze_in, squeeze_out, sampler_kernel, readout_kernel, frame_clip, clip_keep, token_cotangent):
    V = pltpu.VMEM
    dma = pltpu.SemaphoreType.DMA
    scratch = [
        V((2, 144, 196), BF),
        V((9, 48, 144), BF),
        V((144, 144), BF),
        V((18, 1024), BF),
        V((32, 16, 1408), BF),
        V((32, 16, 1152), BF),
        V((128, 1152), BF),
        V((128, 1024), BF),
        V((512, 128), F32),
        V((512, 128), F32),
        V((2, 64, 1024), BF),
        V((9, 256, 256), BF),
        V((3, 2, 288, 256), BF),
        V((2, 256, 256), F32),
        V((2, 256, 256), F32),
        V((2, 256, 256), F32),
        V((256, 256), F32),
        V((2, 256, 256), F32),
        V((256, 288), BF),
        V((256, 288), BF),
        V((8, 256), F32),
        V((NT, 1, 768), F32),
        V((NT, 1, 768), F32),
        V((128, 640), BF),
        V((128, 640), BF),
        V((64, 640), BF),
        V((8, 16, 640), BF),
        V((8, 16, 640), BF),
        V((8, 16, 640), BF),
        V((8, 16, 640), BF),
        V((16, 1, 640), F32),
        V((16, 1, 640), F32),
        V((16, 1, 640), F32),
        V((16, 1, 640), F32),
        V((8, 16, 640), BF),
        V((8, 16, 640), BF),
        V((128, 1152), F32),
        V((64, 640), BF),
        V((64, 640), BF),
        V((2, 64, 640), BF),
        V((2, 64, 640), BF),
        V((64, 1024), BF),
        V((64, 1024), BF),
        dma((7,)),
        dma((2,)),
        dma((1,)), dma((32,)),
        dma((1,)), dma((32,)),
        dma((8, 2)),
        dma((2,)),
        dma((2,)), dma((2,)),
        dma((2,)),
        dma((2,)), dma((2,)),
        dma((2,)),
    ]
    spec = pl.BlockSpec(memory_space=pltpu.VMEM)
    hbm = pl.BlockSpec(memory_space=pltpu.HBM)
    llm_tokens, grad_features = pl.pallas_call(
        kernel,
        out_shape=(jax.ShapeDtypeStruct((64, 1024), BF), jax.ShapeDtypeStruct((2, 144, 196), BF)),
        in_specs=[hbm] * 6 + [spec] * 2 + [hbm],
        out_specs=(spec, spec),
        scratch_shapes=scratch,
        compiler_params=pltpu.CompilerParams(
            collective_id=0, has_side_effects=True, vmem_limit_bytes=62 * 1024 * 1024
        ),
        cost_estimate=pl.CostEstimate(flops=3_000_000_000, bytes_accessed=1_000_000, transcendentals=1_000_000),
        name="connector",
    )(
        features.transpose(0, 2, 1),
        group_kernel.transpose(0, 2, 1),
        squeeze_in,
        squeeze_out.T,
        sampler_kernel.reshape(144, 144),
        readout_kernel,
        frame_clip.reshape(1, 128),
        clip_keep.reshape(1, 16),
        token_cotangent,
    )
    return llm_tokens, grad_features.transpose(0, 2, 1)


def solution(mesh):
    placed = (
        P("ctx", None, "tp"),
        P(None, "tp", None),
        P("tp", None),
        P(None, "tp"),
        P("ctx", None, "tp"),
        P("ctx", "tp"),
        P(),
        P(),
        P("ctx", "tp"),
    )
    return jax.shard_map(
        per_device,
        mesh=mesh,
        in_specs=placed,
        out_specs=(P("ctx", "tp"), P("ctx", None, "tp")),
        check_vma=False,
    )
```

```python
import jax
import jax.numpy as jnp
from jax import lax
from jax.experimental import pallas as pl
from jax.experimental.pallas import tpu as pltpu
from jax.sharding import PartitionSpec as P

NX, NZ, NT = 4, 8, 8
BF = jnp.bfloat16
F32 = jnp.float32
MESH = pl.DeviceIdType.MESH
SLOT = (0, 128, 256, 384, 640, 768, 896, 1024)


def iota(shape, dim):
    return lax.broadcasted_iota(jnp.int32, shape, dim)


def select(hit):
    return jnp.where(hit, 1.0, 0.0).astype(BF)


def mm(a, b):
    return jnp.dot(a, b, preferred_element_type=F32)


def mmt(a, b):
    return lax.dot_general(a, b, (((1,), (1,)), ((), ())), preferred_element_type=F32)


def exact(dot, value, weight):
    high = value.astype(BF)
    left = value - high.astype(F32)
    middle = left.astype(BF)
    low = (left - middle.astype(F32)).astype(BF)
    return dot(high, weight) + (dot(middle, weight) + dot(low, weight))


def sigmoid(v):
    return jax.nn.sigmoid(v)


def slope(v):
    s = sigmoid(v)
    return s * (1.0 + v * (1.0 - s))


def padded_place(cell):
    row = (cell * 4682) >> 16
    return (row + 1) * 16 + (cell - 14 * row) + 1


def token_at(row):
    return 4 * (row & 15) + 2 * ((row >> 4) & 1) + ((row >> 5) & 1)


def patch_place(r):
    s = r >> 6
    token = token_at(r & 63)
    a = token >> 3
    b = token & 7
    return (2 * a + (s >> 1)) * 16 + 2 * b + (s & 1)


def third(v):
    return (v >= 48).astype(jnp.int32) + (v >= 96).astype(jnp.int32)


def kernel(
    feat_h, gk_h, sqi_h, sqo_h, samp_h, read_h, fclip, keep, cot_h,
    llm, gout,
    feat, gk, samp, read,
    sall, rall, srest, rrest, fta, ftb, cotb, wc, xs, cv, ac, sl, bm, gh, sqie, sqoe, pbuf, psl, psl2,
    p0, p1, obuf, prep, rsp, gap, rsg, gas, gad, acs, acd, gpf, acf, gpt, ges, ger, gos, gor, tks, tkr,
    load, cot_sem, s_out, s_in, r_out, r_in, pair, e_sem, o_s, o_r, ge_sem, go_s, go_r, tk_sem,
):
    ctx = lax.axis_index("ctx")
    t = lax.axis_index("tp")
    k = lax.rem(ctx, 2)
    m = lax.div(ctx, 2)
    z = lax.rem(m, NZ)
    x = lax.div(m, NZ)
    chips = NX * NZ

    def dev(xx, zz, kk, tt):
        return ((xx * NZ + zz) * 2 + kk, tt)

    def chip(mm_, kk):
        return (lax.rem(mm_ + chips, chips) * 2 + kk, t)

    def zdev(d):
        return dev(x, lax.rem(z + d + NZ, NZ), k, t)

    def xdev(d):
        return dev(lax.rem(x + d + NX, NX), z, k, t)

    def tdev(d):
        return (ctx, lax.rem(t + d, NT))

    sibling = (m * 2 + (1 - k), t)
    twist = lax.rem(m + lax.div(t, 4), 2)
    row_slot = lax.div(m, 2)
    is_self = (t < 4).astype(jnp.int32)

    def frame_chunk(o):
        return 4 * lax.rem(o, 2) + 2 * lax.rem(lax.div(o, 2), 2) + lax.rem(lax.div(o, 4) + m, 2)

    def decoder_chunk(o):
        return 4 * lax.rem(lax.div(o, 2), 2) + 2 * lax.rem(o, 2) + lax.rem(lax.div(o, 4) + m, 2)

    def row_dev(i):
        return ((2 * i + twist) * 2 + k, t)

    def remote(src, dst, send, recv, where):
        return pltpu.make_async_remote_copy(
            src_ref=src, dst_ref=dst, send_sem=send, recv_sem=recv, device_id=where, device_id_type=MESH
        )

    def exchange(source, slots, slot, which):
        for d in (4, 3, 5, 2, 6, 1, 7):
            o = lax.rem(t + d, NT)
            remote(source(o), slots.at[slot], pair.at[which, 0], pair.at[which, 1], tdev(d)).start()
        all_of = remote(slots.at[0 : NT - 1], slots.at[0 : NT - 1], pair.at[which, 0], pair.at[which, 1], tdev(1))
        leaving.append(all_of.wait_send)
        return all_of.wait_recv

    leaving = []
    coming = {}

    def start(copy):
        copy.start()
        leaving.append(copy.wait_send)

    def arrive(*names):
        for name in names:
            coming.pop(name)()

    def finish():
        arrive(*list(coming))
        for left in leaving:
            left()

    barrier = pltpu.get_barrier_semaphore()

    def hello(where):
        pl.semaphore_signal(barrier, inc=1, device_id=where, device_id_type=MESH)

    local = []
    for i, (src, dst) in enumerate(
        (
            (read_h, read), (samp_h, samp), (feat_h, feat), (gk_h, gk), (cot_h, cotb.at[k]),
            (sqi_h, sqie.at[0:144]), (sqo_h, sqoe.at[0:144]),
        )
    ):
        local.append(pltpu.make_async_copy(src, dst, load.at[i]))
        local[-1].start()

    hello(sibling)
    for d in range(1, NX):
        hello(xdev(d))
    hello(zdev(1))
    hello(zdev(-1))
    for d in range(1, NT):
        hello(tdev(d))
    hello(chip(m - 1, 1))

    @pl.when(k == 1)
    def _():
        hello(chip(m + 1, 0))
        hello(chip(m + 1, 1))

    trade = [lax.rem(row_slot + j, 16) for j in range(16)]

    @pl.when(is_self == 0)
    def _():
        hello(row_dev(trade[0]))

    for j in range(1, 16):
        hello(row_dev(trade[j]))

    own = 4 * z + x
    local[0].wait()
    rall[own, :, 0:1024] = read[0:16, :]
    last = read[16:18, :].astype(F32)
    for j in range(2):
        for p in range(8):
            fta[256 + j * 8 + p : 257 + j * 8 + p, :] = last[j : j + 1, 128 * p : 128 * p + 128]
    rall[own, :, 1024:1152] = fta[256:272, :].astype(BF)
    local[1].wait()
    ftb[0:144, :] = jnp.zeros((144, 128), F32)
    fta[0:144, :] = samp[:, 0:128].astype(F32)
    ftb[0:144, 0:16] = samp[:, 128:144].astype(F32)
    rest = jnp.zeros((16, 128), F32)
    for s in range(8):
        sall[own, :, SLOT[s] : SLOT[s] + 128] = fta[pl.ds(s, 16, stride=8), :].astype(BF)
        tail = ftb[pl.ds(s, 16, stride=8), :]
        rest = rest + (tail if s == 0 else pltpu.roll(tail, 16 * s, 1))
    sall[own, :, 512:640] = rest.astype(BF)
    sall[own, :, 1152:1280] = fta[128:144, :].astype(BF)
    sall[own, :, 1280:1408] = ftb[128:144, :].astype(BF)

    pl.semaphore_wait(barrier, 1 + (NX - 1) + 2 + (NT - 1) + (1 + 2 * k) + 16 - is_self)

    def zi(d):
        return lax.rem(z + d + NZ, NZ)

    def xi(e):
        return lax.rem(x + e, NX)

    def hop(d):
        return {-1: 0, -2: 1, -3: 2, 1: 3, 2: 4, 3: 5, 4: 6}[d]

    class Gather:
        def __init__(self, ref, out, into, way):
            self.ref, self.out, self.into, self.way = ref, out, into, way

        def block(self, d, e):
            return self.ref.at[4 * zi(d) + xi(e)]

        def send(self, d, e, sem, where):
            remote(self.block(d, e), self.block(d, e), self.out.at[0], self.into.at[sem], where).start()

        def got(self, d, e, sem):
            remote(self.block(d, e), self.block(d, e), self.out.at[0], self.into.at[sem], sibling).wait_recv()

        def a_z(self, e):
            if e:
                self.got(0, e, e)
            self.send(0, e, 4 + 7 * e + hop(-1), zdev(1))
            self.send(0, e, 4 + 7 * e + hop(1), zdev(-1))

        def a_start(self):
            for e in (1, 3, 2):
                self.send(0, 0, (-e) % 4, xdev(e))
            self.a_z(0)

        def a_ring(self, i, *columns):
            for e in columns:
                at = 4 + 7 * e
                self.got(-i, e, at + hop(-i))
                self.got(i, e, at + hop(i))
                if i < 3:
                    self.send(-i, e, at + hop(-i - 1), zdev(1))
                    self.send(i, e, at + hop(i + 1), zdev(-1))
                else:
                    way = 1 if e % 2 == 0 else -1
                    self.send(-3 * way, e, at + hop(4), zdev(way))

        def a_end(self):
            for e in (0, 1, 3, 2):
                self.got(4, e, 4 + 7 * e + hop(4))

        def b_at(self, d, e):
            return 7 + 3 * (d % 8) + e - 1

        def b_x(self, d):
            self.send(d, 0, self.b_at(d, 3), xdev(1))
            self.send(d, 0, self.b_at(d, 1), xdev(-1))

        def b_start(self):
            self.send(0, 0, hop(-1), zdev(1))
            self.send(0, 0, hop(1), zdev(-1))
            self.b_x(0)

        def b_ring(self, i):
            if i == 4:
                self.got(4, 0, hop(4))
                self.b_x(4)
                return
            self.got(-i, 0, hop(-i))
            self.got(i, 0, hop(i))
            if i < 3:
                self.send(-i, 0, hop(-i - 1), zdev(1))
                self.send(i, 0, hop(i + 1), zdev(-1))
            else:
                self.send(-3 * self.way, 0, hop(4), zdev(self.way))
            self.b_x(-i)
            self.b_x(i)

        def b_pass(self, *rows):
            for d in rows:
                e = 3 if d % 2 == 0 else 1
                self.got(d, e, self.b_at(d, e))
                self.send(d, e, self.b_at(d, 2), xdev(1 if e == 3 else -1))

        def b_end(self):
            for d in (0, 1, -1, 2, -2, 3, -3, 4):
                e = 1 if d % 2 == 0 else 3
                self.got(d, e, self.b_at(d, e))
            for d in (0, 1, -1, 2, -2, 3, -3, 4):
                self.got(d, 2, self.b_at(d, 2))

        def end(self):
            cores(self.a_end, self.b_end)

    def cores(zero, one):
        pl.when(k == 0)(lambda: zero() and None)
        pl.when(k == 1)(lambda: one() and None)

    R = Gather(rall, r_out, r_in, 1)
    S = Gather(sall, s_out, s_in, -1)

    def weights_sent():
        remote(rall.at[0:31], rall.at[0:31], r_out.at[0], r_out.at[0], sibling).wait_send()
        remote(sall.at[0:31], sall.at[0:31], s_out.at[0], s_out.at[0], sibling).wait_send()

    leaving.append(weights_sent)

    def pump(n):
        cores(
            [
                lambda: (R.a_start(), S.a_start()),
                lambda: (R.a_z(1), R.a_z(3), R.a_z(2)),
                lambda: (R.a_ring(1, 0), S.a_z(1), S.a_z(3)),
                lambda: (R.a_ring(1, 1, 3, 2), S.a_z(2)),
                lambda: (R.a_ring(2, 0), S.a_ring(1, 0)),
                lambda: (R.a_ring(2, 1, 3, 2), S.a_ring(1, 1)),
                lambda: (R.a_ring(3, 0), S.a_ring(1, 3, 2)),
                lambda: (R.a_ring(3, 1, 3, 2), S.a_ring(2, 0)),
                lambda: S.a_ring(2, 1, 3),
                lambda: S.a_ring(2, 2),
                lambda: S.a_ring(3, 0),
                lambda: S.a_ring(3, 1, 3),
                lambda: S.a_ring(3, 2),
            ][n],
            [
                lambda: (R.b_start(), S.b_start()),
                lambda: R.b_ring(1),
                lambda: (R.b_ring(2), S.b_ring(1)),
                lambda: (R.b_ring(3), R.b_pass(0)),
                lambda: (S.b_ring(2), R.b_ring(4), R.b_pass(1, -1)),
                lambda: (R.b_pass(2, -2), S.b_pass(0)),
                lambda: (R.b_pass(3, -3, 4), S.b_ring(3)),
                lambda: (S.b_pass(1, -1), S.b_ring(4)),
                lambda: S.b_pass(2),
                lambda: S.b_pass(-2),
                lambda: S.b_pass(3),
                lambda: S.b_pass(-3, 4),
                lambda: None,
            ][n],
        )

    pump(0)
    start(remote(cot_h, cotb.at[k], cot_sem.at[0], cot_sem.at[1], sibling))
    coming["cot"] = remote(cot_h, cotb.at[1 - k], cot_sem.at[0], cot_sem.at[1], sibling).wait_recv
    cell = iota((256, 256), 0)
    cy, cx = cell >> 4, cell & 15
    inside = jnp.logical_and(
        jnp.logical_and(cy >= 1, cy <= 14), jnp.logical_and(cx >= 1, cx <= 14)
    )
    bm[...] = jnp.where(inside, 1.0, 0.0)
    into = select(padded_place(iota((256, 196), 1)) == iota((256, 196), 0))
    channel = iota((144, 48), 0)
    spread = select(channel - 48 * third(channel) == iota((144, 48), 1))
    same_group = third(iota((144, 144), 0)) == third(iota((144, 144), 1))
    blank = jnp.zeros((112, 196), BF)

    def centre(f):
        if f == 0:
            local[2].wait()
        return mmt(into, jnp.concatenate([feat[f], blank], axis=0))

    def put_shifts(f, value):
        xs[0, f, 16:272, :] = pltpu.roll(value, 1, 0).astype(BF)
        xs[1, f, 16:272, :] = value.astype(BF)
        xs[2, f, 16:272, :] = pltpu.roll(value, 255, 0).astype(BF)

    for f in range(2):
        for j in range(3):
            xs[j, f, 0:16, :] = jnp.zeros((16, 256), BF)
            xs[j, f, 272:288, :] = jnp.zeros((16, 256), BF)
        put_shifts(f, centre(f))
        pump(1 + f)
    local[3].wait()
    for tap in range(9):
        wc[tap] = jnp.zeros((256, 256), BF)
        dense = jnp.where(same_group, mm(spread, gk[tap]), 0.0)
        wc[tap, 0:144, 0:144] = dense.astype(BF)
        if tap == 4:
            pump(3)
    sqoe[144:256, :] = jnp.zeros((112, 288), BF)
    sqie[144:256, :] = jnp.zeros((112, 288), BF)
    pbuf[...] = jnp.zeros((8, 256), F32)
    pump(4)

    both = jnp.zeros((512, 256), F32)
    for dy in range(3):
        for dx in range(3):
            window = xs[dx, :, 16 * dy : 16 * dy + 256, :].reshape(512, 256)
            both = both + mmt(window, wc[3 * dy + dx])
        pump(5 + dy)
    for f in range(2):
        total = both[256 * f : 256 * f + 256]
        cv[f] = total
        act = total * sigmoid(total) * bm[...]
        ac[f] = act
        pbuf[f : f + 1, :] = jnp.sum(act, axis=0, keepdims=True) * (1.0 / 196.0)
    local[5].wait()
    local[6].wait()

    def put_sums(slots, sums, which):
        slots[t] = jnp.zeros((1, 768), F32)
        slots[t, :, 0:288] = sums[0:1]
        slots[t, :, 384:672] = sums[1:2]
        return exchange(lambda o: slots.at[t], slots, t, which)

    def get_sums(slots):
        both_rows = jnp.sum(slots[...], axis=0)
        return jnp.concatenate([both_rows[:, 0:288], both_rows[:, 384:672], jnp.zeros((6, 288), F32)], axis=0)

    coming["ps"] = put_sums(psl, exact(mm, pbuf[...], sqie[...]), 0)
    pump(8)

    clips = fclip[...].astype(F32)
    lane = iota((64, 128), 1)
    clip_col = jnp.sum(jnp.where(lane == 2 * token_at(iota((64, 128), 0)), clips, 0.0), axis=1, keepdims=True)
    before = jnp.logical_and((lane & 1) == 0, clips < clip_col)
    first = jnp.sum(jnp.where(before, 1.0, 0.0), axis=1, keepdims=True)
    lane16 = iota((64, 16), 1).astype(F32)
    kept = jnp.sum(jnp.where(lane16 == clip_col, keep[...].astype(F32), 0.0), axis=1, keepdims=True)
    place = (token_at(iota((64, 1), 0)).astype(F32) - first) * 64.0

    def live(d):
        return jnp.where(place + jnp.asarray(d, jnp.int32).astype(F32) < kept, 1.0, 0.0)

    lane1 = iota((1, 128), 1)

    def pair_mask(c):
        now = jnp.sum(jnp.where(lane1 == 2 * c, clips, 0.0), axis=1, keepdims=True)
        was = jnp.sum(jnp.where(lane1 == 2 * c - 1, clips, 0.0), axis=1, keepdims=True)
        return jnp.where(jnp.logical_and(now == was, iota((1, 1), 0) + c > 0), 1.0, 0.0)

    mask0, mask1 = pair_mask(2 * m), pair_mask(2 * m + 1)

    for f in range(2):
        sl[f] = slope(cv[f]) * bm[...]
        pump(9 + f)

    arrive("ps")
    squeezed = get_sums(psl)
    excite = sigmoid(exact(mmt, squeezed * sigmoid(squeezed), sqoe[...]))
    other = pl.ds(pl.multiple_of(64 * (1 - k), 64), 64)
    gather = select(patch_place(iota((256, 256), 0)) == iota((256, 256), 1))
    for f in range(2):
        hidden = xs[1, f, 16:272, :].astype(F32) + ac[f] * excite[f : f + 1, :]
        taps = mm(gather, hidden.astype(BF))
        base = 4 * (1 - f)
        rest = jnp.zeros((64, 128), F32)
        for s in range(4):
            tail = taps[64 * s : 64 * s + 64, 128:256]
            by = 16 * (s + base)
            rest = rest + (tail if by == 0 else pltpu.roll(tail, by, 1))
        main = taps[:, 0:128].astype(BF)
        if f == 0:
            mine = pl.ds(pl.multiple_of(64 * k, 64), 64)
            p1[mine, 0:128] = rest.astype(BF)
            for s in range(4):
                p1[mine, 128 * (s + 1) : 128 * (s + 2)] = main[64 * s : 64 * s + 64]
            start(remote(p1.at[mine], p1.at[mine], e_sem.at[0], e_sem.at[1], sibling))
            coming["even"] = lambda: remote(p1.at[other], p1.at[other], e_sem.at[0], e_sem.at[1], sibling).wait_recv()
        else:
            obuf[:, 512:640] = rest.astype(BF)
            for s in range(4):
                obuf[:, 128 * s : 128 * (s + 1)] = main[64 * s : 64 * s + 64]

    def send_odd():
        @pl.when(k == 0)
        def _():
            p0[64:128, :] = obuf[...]
            remote(obuf, p0.at[64:128], o_s.at[0], o_r.at[1], sibling).start()

        @pl.when(k == 1)
        def _():
            remote(obuf, p0.at[0:64], o_s.at[0], o_r.at[0], chip(m + 1, 1)).start()
            remote(obuf, p0.at[0:64], o_s.at[1], o_r.at[0], chip(m + 1, 0)).start()

    def odd_sent():
        remote(obuf, p0.at[0:64], o_s.at[0], o_r.at[0], sibling).wait_send()

        @pl.when(k == 1)
        def _():
            remote(obuf, p0.at[0:64], o_s.at[1], o_r.at[0], sibling).wait_send()

    def odd_here():
        remote(obuf, p0.at[0:64], o_s.at[0], o_r.at[0], sibling).wait_recv()

        @pl.when(k == 1)
        def _():
            remote(obuf, p0.at[64:128], o_s.at[0], o_r.at[1], sibling).wait_recv()

    send_odd()
    leaving.append(odd_sent)
    coming["odd"] = odd_here

    local[4].wait()
    R.end()
    fta[...] = rall[:, :, 1024:1152].reshape(512, 128).astype(F32)
    for p in range(8):
        rrest[0:64, 128 * p : 128 * p + 128] = fta[pl.ds(p, 64, stride=8), :].astype(BF)
    rrest[64:128, :] = jnp.zeros((64, 1024), BF)
    arrive("cot")
    order = select(token_at(iota((64, 64), 0)) == iota((64, 64), 1))
    back = jnp.concatenate([mm(order, cotb[0]).astype(BF), mm(order, cotb[1]).astype(BF)], axis=0)
    alive = jnp.concatenate([live(2 * m), live(2 * m + 1)], axis=0)
    gap[:, :, 0:512] = (
        (mmt(back, rall[:, :, 0:1024].reshape(512, 1024)) * alive).astype(BF).reshape(8, 16, 512)
    )
    pump(11)
    gap[:, :, 512:640] = (mmt(back, rrest[...]) * alive).astype(BF).reshape(8, 16, 128)

    def scattered(parts, chunk, slots):
        total = parts[chunk].astype(F32)
        for d in range(1, NT):
            total = total + slots[lax.rem(t + d, NT)].astype(F32)
        return total

    coming["rg"] = exchange(lambda o: gap.at[decoder_chunk(o)], rsg, t, 1)
    pump(12)

    def put_rows(src, value, dst, which):
        for i in range(16):
            src[i] = value[i : i + 1, :]

        @pl.when(is_self == 1)
        def _():
            dst[row_slot] = src[row_slot]

        @pl.when(is_self == 0)
        def _():
            i = trade[0]
            remote(src.at[i], dst.at[row_slot], pair.at[which, 0], pair.at[which, 1], row_dev(i)).start()

        for i in [trade[j] for j in (10, 6, 14, 2, 9, 11, 5, 7, 13, 15, 1, 3, 8, 4, 12)]:
            remote(src.at[i], dst.at[row_slot], pair.at[which, 0], pair.at[which, 1], row_dev(i)).start()

        def both(wait):
            @pl.when(is_self == 1)
            def _():
                wait(remote(src.at[0:15], dst.at[0:15], pair.at[which, 0], pair.at[which, 1], sibling))

            @pl.when(is_self == 0)
            def _():
                wait(remote(src, dst, pair.at[which, 0], pair.at[which, 1], sibling))

        leaving.append(lambda: both(lambda copy: copy.wait_send()))
        return lambda: both(lambda copy: copy.wait_recv())

    def get_rows(dst):
        return jnp.concatenate([dst[i] for i in range(16)], axis=0)

    arrive("even", "odd")
    S.end()
    fta[...] = sall[:, :, 1152:1280].reshape(512, 128).astype(F32)
    ftb[...] = sall[:, :, 1280:1408].reshape(512, 128).astype(F32)
    rest = jnp.zeros((64, 128), F32)
    for s in range(8):
        srest[0:64, SLOT[s] : SLOT[s] + 128] = fta[pl.ds(s, 64, stride=8), :].astype(BF)
        tail = ftb[pl.ds(s, 64, stride=8), :]
        rest = rest + (tail if s == 0 else pltpu.roll(tail, 16 * s, 1))
    srest[0:64, 512:640] = rest.astype(BF)
    srest[64:128, :] = jnp.zeros((64, 1152), BF)

    mask_col = jnp.concatenate(
        [jnp.broadcast_to(mask0, (64, 1)), jnp.broadcast_to(mask1, (64, 1))], axis=0
    )

    def pre_part(w0, w1):
        return mmt(p0[...], w0) * mask_col + mmt(p1[...], w1)

    prep[:, :, 0:512] = (
        pre_part(sall[:, :, 0:640].reshape(512, 640), sall[:, :, 512:1152].reshape(512, 640))
        .astype(BF)
        .reshape(8, 16, 512)
    )
    prep[:, :, 512:640] = pre_part(srest[:, 0:640], srest[:, 512:1152]).astype(BF).reshape(8, 16, 128)
    coming["rp"] = exchange(lambda o: prep.at[frame_chunk(o)], rsp, t, 2)

    arrive("rg")
    coming["ga"] = put_rows(gas, scattered(gap, decoder_chunk(t), rsg), gad, 3)
    arrive("rp")
    pre = scattered(prep, frame_chunk(t), rsp)
    pre_slope = slope(pre)
    arrive("ga")
    in_frames = frame_chunk(t)
    gpf[in_frames] = (get_rows(gad) * pre_slope).astype(BF)
    coming["gp"] = exchange(lambda o: gpf.at[in_frames], gpf, in_frames, 5)
    coming["aa"] = put_rows(acs, (pre * sigmoid(pre)).astype(BF).astype(F32), acd, 4)
    arrive("gp")
    grads = gpf[...].reshape(128, 640)
    def grad_taps(lanes):
        gpt[:, lanes] = mm(grads[:, 0:512], sall[:, :, lanes].reshape(512, lanes.stop - lanes.start)) + mm(grads[:, 512:640], srest[:, lanes])

    grad_taps(slice(0, 640))
    gos[0] = (gpt[0:64, 0:640] * mask0).astype(BF)
    start(remote(gos.at[0], gor.at[k], go_s.at[0], go_r.at[k], chip(m - 1, 1)))
    gos[1] = (gpt[64:128, 0:640] * mask1).astype(BF)

    @pl.when(k == 1)
    def _():
        remote(gos.at[1], gor.at[1], go_s.at[1], go_r.at[1], sibling).start()

    @pl.when(k == 0)
    def _():
        gor[0] = gos[1]

    def grad_odd_sent():
        @pl.when(k == 1)
        def _():
            remote(gos.at[1], gor.at[1], go_s.at[1], go_r.at[1], sibling).wait_send()

    def grad_odd_here():
        remote(gos.at[0], gor.at[1], go_s.at[0], go_r.at[1], sibling).wait_recv()

        @pl.when(k == 1)
        def _():
            remote(gos.at[0], gor.at[0], go_s.at[0], go_r.at[0], sibling).wait_recv()

    leaving.append(grad_odd_sent)
    grad_taps(slice(640, 1152))
    ges[...] = gpt[other, 512:1152].astype(BF)
    start(remote(ges, ger, ge_sem.at[0], ge_sem.at[1], sibling))
    coming["ge"] = remote(ges, ger, ge_sem.at[0], ge_sem.at[1], sibling).wait_recv
    coming["go"] = grad_odd_here

    arrive("aa")
    in_decoder = decoder_chunk(t)
    acf[in_decoder] = get_rows(acd).astype(BF)
    coming["af"] = exchange(lambda o: acf.at[in_decoder], acf, in_decoder, 6)

    arrive("ge", "go")
    mine = pl.ds(pl.multiple_of(64 * k, 64), 64)
    even = gpt[mine, 512:1152] + ger[...].astype(F32)
    odd = gor[0].astype(F32) + gor[1].astype(F32)
    ungather = select(patch_place(iota((256, 256), 1)) == iota((256, 256), 0))
    narrow = iota((64, 128), 1) < 16
    for f in range(2):
        if f == 0:
            tile, mains, base = even[:, 0:128], even[:, 128:640], 4
        else:
            tile, mains, base = odd[:, 512:640], odd[:, 0:512], 0
        main = jnp.concatenate([mains[:, 128 * s : 128 * s + 128] for s in range(4)], axis=0)
        tails = []
        for s in range(4):
            by = (128 - 16 * (s + base)) % 128
            tails.append(jnp.where(narrow, tile if by == 0 else pltpu.roll(tile, by, 1), 0.0))
        taps = jnp.concatenate([main, jnp.concatenate(tails, axis=0)], axis=1)
        top = taps.astype(BF)
        bottom = (taps - top.astype(F32)).astype(BF)
        grad = (mm(ungather, top) + mm(ungather, bottom)) * bm[...]
        gh[f] = grad
        pbuf[f : f + 1, :] = jnp.sum(grad * ac[f], axis=0, keepdims=True)

    inner = pbuf[...] * excite * (1.0 - excite)
    coming["pq"] = put_sums(psl2, exact(mm, inner, sqoe[...]), 7)
    arrive("af")
    acts = acf[...].reshape(128, 640)
    part = mm(acts[:, 0:512], rall[:, :, 0:1024].reshape(512, 1024)) + mm(acts[:, 512:640], rrest[...])
    low, high = part[0:64], part[64:128]
    kf = k.astype(F32)
    tks[...] = (low * kf + high * (1.0 - kf)).astype(BF)
    start(remote(tks, tkr, tk_sem.at[0], tk_sem.at[1], sibling))
    own_tokens = low * (1.0 - kf) + high * kf
    coming["tk"] = remote(tks, tkr, tk_sem.at[0], tk_sem.at[1], sibling).wait_recv

    arrive("pq")
    grad_squeezed = get_sums(psl2) * slope(squeezed)
    grad_pooled = exact(mmt, grad_squeezed, sqie[...]) * (1.0 / 196.0)
    outof = select(padded_place(iota((196, 256), 0)) == iota((196, 256), 1))
    for f in range(2):
        grad_active = gh[f] * excite[f : f + 1, :] + grad_pooled[f : f + 1, :]
        put_shifts(f, grad_active * sl[f])
    both = gh[...].reshape(512, 256)
    for dy in range(3):
        for dx in range(3):
            window = xs[2 - dx, :, 16 * (2 - dy) : 16 * (2 - dy) + 256, :].reshape(512, 256)
            both = both + mm(window, wc[3 * dy + dx])
    for f in range(2):
        turned = both[256 * f : 256 * f + 256].T[0:144].astype(BF)
        gout[f] = mmt(turned, outof).astype(BF)

    arrive("tk")
    rows = ((own_tokens + tkr[...].astype(F32)) * live(ctx)).astype(BF)
    llm[...] = mm(select(token_at(iota((64, 64), 1)) == iota((64, 64), 0)), rows).astype(BF)
    finish()


def per_device(features, group_kernel, squeeze_in, squeeze_out, sampler_kernel, readout_kernel, frame_clip, clip_keep, token_cotangent):
    V = pltpu.VMEM
    dma = pltpu.SemaphoreType.DMA
    scratch = [
        V((2, 144, 196), BF),
        V((9, 48, 144), BF),
        V((144, 144), BF),
        V((18, 1024), BF),
        V((32, 16, 1408), BF),
        V((32, 16, 1152), BF),
        V((128, 1152), BF),
        V((128, 1024), BF),
        V((512, 128), F32),
        V((512, 128), F32),
        V((2, 64, 1024), BF),
        V((9, 256, 256), BF),
        V((3, 2, 288, 256), BF),
        V((2, 256, 256), F32),
        V((2, 256, 256), F32),
        V((2, 256, 256), F32),
        V((256, 256), F32),
        V((2, 256, 256), F32),
        V((256, 288), BF),
        V((256, 288), BF),
        V((8, 256), F32),
        V((NT, 1, 768), F32),
        V((NT, 1, 768), F32),
        V((128, 640), BF),
        V((128, 640), BF),
        V((64, 640), BF),
        V((8, 16, 640), BF),
        V((8, 16, 640), BF),
        V((8, 16, 640), BF),
        V((8, 16, 640), BF),
        V((16, 1, 640), F32),
        V((16, 1, 640), F32),
        V((16, 1, 640), F32),
        V((16, 1, 640), F32),
        V((8, 16, 640), BF),
        V((8, 16, 640), BF),
        V((128, 1152), F32),
        V((64, 640), BF),
        V((64, 640), BF),
        V((2, 64, 640), BF),
        V((2, 64, 640), BF),
        V((64, 1024), BF),
        V((64, 1024), BF),
        dma((7,)),
        dma((2,)),
        dma((1,)), dma((32,)),
        dma((1,)), dma((32,)),
        dma((8, 2)),
        dma((2,)),
        dma((2,)), dma((2,)),
        dma((2,)),
        dma((2,)), dma((2,)),
        dma((2,)),
    ]
    spec = pl.BlockSpec(memory_space=pltpu.VMEM)
    hbm = pl.BlockSpec(memory_space=pltpu.HBM)
    llm_tokens, grad_features = pl.pallas_call(
        kernel,
        out_shape=(jax.ShapeDtypeStruct((64, 1024), BF), jax.ShapeDtypeStruct((2, 144, 196), BF)),
        in_specs=[hbm] * 6 + [spec] * 2 + [hbm],
        out_specs=(spec, spec),
        scratch_shapes=scratch,
        compiler_params=pltpu.CompilerParams(
            collective_id=0, has_side_effects=True, vmem_limit_bytes=62 * 1024 * 1024
        ),
        cost_estimate=pl.CostEstimate(flops=3_000_000_000, bytes_accessed=1_000_000, transcendentals=1_000_000),
        name="connector",
    )(
        features.transpose(0, 2, 1),
        group_kernel.transpose(0, 2, 1),
        squeeze_in,
        squeeze_out.T,
        sampler_kernel.reshape(144, 144),
        readout_kernel,
        frame_clip.reshape(1, 128),
        clip_keep.reshape(1, 16),
        token_cotangent,
    )
    return llm_tokens, grad_features.transpose(0, 2, 1)


def solution(mesh):
    placed = (
        P("ctx", None, "tp"),
        P(None, "tp", None),
        P("tp", None),
        P(None, "tp"),
        P("ctx", None, "tp"),
        P("ctx", "tp"),
        P(),
        P(),
        P("ctx", "tp"),
    )
    return jax.shard_map(
        per_device,
        mesh=mesh,
        in_specs=placed,
        out_specs=(P("ctx", "tp"), P("ctx", None, "tp")),
        check_vma=False,
    )
```

```python
import jax
import jax.numpy as jnp
from jax import lax
from jax.experimental import pallas as pl
from jax.experimental.pallas import tpu as pltpu
from jax.sharding import PartitionSpec as P

NX, NZ, NT = 4, 8, 8
BF = jnp.bfloat16
F32 = jnp.float32
MESH = pl.DeviceIdType.MESH
SLOT = (0, 128, 256, 384, 640, 768, 896, 1024)


def iota(shape, dim):
    return lax.broadcasted_iota(jnp.int32, shape, dim)


def select(hit):
    return jnp.where(hit, 1.0, 0.0).astype(BF)


def mm(a, b):
    return jnp.dot(a, b, preferred_element_type=F32)


def mmt(a, b):
    return lax.dot_general(a, b, (((1,), (1,)), ((), ())), preferred_element_type=F32)


def exact(dot, value, weight):
    high = value.astype(BF)
    left = value - high.astype(F32)
    middle = left.astype(BF)
    low = (left - middle.astype(F32)).astype(BF)
    return dot(high, weight) + (dot(middle, weight) + dot(low, weight))


def sigmoid(v):
    return jax.nn.sigmoid(v)


def slope(v):
    s = sigmoid(v)
    return s * (1.0 + v * (1.0 - s))


def padded_place(cell):
    row = (cell * 4682) >> 16
    return (row + 1) * 16 + (cell - 14 * row) + 1


def token_at(row):
    return 4 * (row & 15) + 2 * ((row >> 4) & 1) + ((row >> 5) & 1)


def patch_place(r):
    s = r >> 6
    token = token_at(r & 63)
    a = token >> 3
    b = token & 7
    return (2 * a + (s >> 1)) * 16 + 2 * b + (s & 1)


def third(v):
    return (v >= 48).astype(jnp.int32) + (v >= 96).astype(jnp.int32)


def kernel(
    feat_h, gk_h, sqi_h, sqo_h, samp_h, read_h, fclip, keep, cot_h,
    llm, gout,
    feat, gk, samp, read,
    sall, rall, srest, rrest, fta, ftb, cotb, wc, xs, cv, ac, sl, bm, gh, sqie, sqoe, pbuf, psl, psl2,
    p0, p1, obuf, prep, rsp, gap, rsg, gas, gad, acs, acd, gpf, acf, gpt, ges, ger, gos, gor, tks, tkr,
    load, cot_sem, s_out, s_in, r_out, r_in, pair, e_sem, o_s, o_r, ge_sem, go_s, go_r, tk_sem,
):
    ctx = lax.axis_index("ctx")
    t = lax.axis_index("tp")
    k = lax.rem(ctx, 2)
    m = lax.div(ctx, 2)
    z = lax.rem(m, NZ)
    x = lax.div(m, NZ)
    chips = NX * NZ

    def dev(xx, zz, kk, tt):
        return ((xx * NZ + zz) * 2 + kk, tt)

    def chip(mm_, kk):
        return (lax.rem(mm_ + chips, chips) * 2 + kk, t)

    def zdev(d):
        return dev(x, lax.rem(z + d + NZ, NZ), k, t)

    def xdev(d):
        return dev(lax.rem(x + d + NX, NX), z, k, t)

    def tdev(d):
        return (ctx, lax.rem(t + d, NT))

    sibling = (m * 2 + (1 - k), t)
    twist = lax.rem(m + lax.div(t, 4), 2)
    row_slot = lax.div(m, 2)
    is_self = (t < 4).astype(jnp.int32)

    def frame_chunk(o):
        return 4 * lax.rem(o, 2) + 2 * lax.rem(lax.div(o, 2), 2) + lax.rem(lax.div(o, 4) + m, 2)

    def decoder_chunk(o):
        return 4 * lax.rem(lax.div(o, 2), 2) + 2 * lax.rem(o, 2) + lax.rem(lax.div(o, 4) + m, 2)

    def row_dev(i):
        return ((2 * i + twist) * 2 + k, t)

    def remote(src, dst, send, recv, where):
        return pltpu.make_async_remote_copy(
            src_ref=src, dst_ref=dst, send_sem=send, recv_sem=recv, device_id=where, device_id_type=MESH
        )

    def exchange(source, slots, slot, which):
        for d in (4, 3, 5, 2, 6, 1, 7):
            o = lax.rem(t + d, NT)
            remote(source(o), slots.at[slot], pair.at[which, 0], pair.at[which, 1], tdev(d)).start()
        all_of = remote(slots.at[0 : NT - 1], slots.at[0 : NT - 1], pair.at[which, 0], pair.at[which, 1], tdev(1))
        leaving.append(all_of.wait_send)
        return all_of.wait_recv

    leaving = []
    coming = {}

    def start(copy):
        copy.start()
        leaving.append(copy.wait_send)

    def arrive(*names):
        for name in names:
            coming.pop(name)()

    def finish():
        arrive(*list(coming))
        for left in leaving:
            left()

    barrier = pltpu.get_barrier_semaphore()

    def hello(where):
        pl.semaphore_signal(barrier, inc=1, device_id=where, device_id_type=MESH)

    local = []
    for i, (src, dst) in enumerate(
        (
            (read_h, read), (samp_h, samp), (feat_h, feat), (gk_h, gk), (cot_h, cotb.at[k]),
            (sqi_h, sqie.at[0:144]), (sqo_h, sqoe.at[0:144]),
        )
    ):
        local.append(pltpu.make_async_copy(src, dst, load.at[i]))
        local[-1].start()

    trade = [lax.rem(row_slot + j, 16) for j in range(16)]

    @pl.when(is_self == 0)
    def _():
        hello(row_dev(trade[0]))

    for j in (10, 6, 14, 2, 9, 11, 5, 7, 13, 15, 1, 3, 8, 4, 12):
        hello(row_dev(trade[j]))
    for d in (4, 3, 5, 2, 6, 1, 7):
        hello(tdev(d))
    for d in (2, 1, 3):
        hello(xdev(d))
    hello(zdev(1))
    hello(zdev(-1))
    hello(sibling)
    hello(chip(m - 1, 1))

    @pl.when(k == 1)
    def _():
        hello(chip(m + 1, 0))
        hello(chip(m + 1, 1))


    own = 4 * z + x
    local[0].wait()
    rall[own, :, 0:1024] = read[0:16, :]
    last = read[16:18, :].astype(F32)
    for j in range(2):
        for p in range(8):
            fta[256 + j * 8 + p : 257 + j * 8 + p, :] = last[j : j + 1, 128 * p : 128 * p + 128]
    rall[own, :, 1024:1152] = fta[256:272, :].astype(BF)
    local[1].wait()
    ftb[0:144, :] = jnp.zeros((144, 128), F32)
    fta[0:144, :] = samp[:, 0:128].astype(F32)
    ftb[0:144, 0:16] = samp[:, 128:144].astype(F32)
    rest = jnp.zeros((16, 128), F32)
    for s in range(8):
        sall[own, :, SLOT[s] : SLOT[s] + 128] = fta[pl.ds(s, 16, stride=8), :].astype(BF)
        tail = ftb[pl.ds(s, 16, stride=8), :]
        rest = rest + (tail if s == 0 else pltpu.roll(tail, 16 * s, 1))
    sall[own, :, 512:640] = rest.astype(BF)
    sall[own, :, 1152:1280] = fta[128:144, :].astype(BF)
    sall[own, :, 1280:1408] = ftb[128:144, :].astype(BF)

    pl.semaphore_wait(barrier, 1 + (NX - 1) + 2 + (NT - 1) + (1 + 2 * k) + 16 - is_self)

    def zi(d):
        return lax.rem(z + d + NZ, NZ)

    def xi(e):
        return lax.rem(x + e, NX)

    def hop(d):
        return {-1: 0, -2: 1, -3: 2, 1: 3, 2: 4, 3: 5, 4: 6}[d]

    class Gather:
        def __init__(self, ref, out, into, way):
            self.ref, self.out, self.into, self.way = ref, out, into, way

        def block(self, d, e):
            return self.ref.at[4 * zi(d) + xi(e)]

        def send(self, d, e, sem, where):
            remote(self.block(d, e), self.block(d, e), self.out.at[0], self.into.at[sem], where).start()

        def got(self, d, e, sem):
            remote(self.block(d, e), self.block(d, e), self.out.at[0], self.into.at[sem], sibling).wait_recv()

        def a_z(self, e):
            if e:
                self.got(0, e, e)
            self.send(0, e, 4 + 7 * e + hop(-1), zdev(1))
            self.send(0, e, 4 + 7 * e + hop(1), zdev(-1))

        def a_start(self):
            for e in (2, 1, 3):
                self.send(0, 0, (-e) % 4, xdev(e))
            self.a_z(0)

        def a_ring(self, i, *columns):
            for e in columns:
                at = 4 + 7 * e
                self.got(-i, e, at + hop(-i))
                self.got(i, e, at + hop(i))
                if i < 3:
                    self.send(-i, e, at + hop(-i - 1), zdev(1))
                    self.send(i, e, at + hop(i + 1), zdev(-1))
                else:
                    way = 1 if e % 2 == 0 else -1
                    self.send(-3 * way, e, at + hop(4), zdev(way))

        def a_end(self):
            for e in (0, 1, 3, 2):
                self.got(4, e, 4 + 7 * e + hop(4))

        def b_at(self, d, e):
            return 7 + 3 * (d % 8) + e - 1

        def b_x(self, d):
            self.send(d, 0, self.b_at(d, 3), xdev(1))
            self.send(d, 0, self.b_at(d, 1), xdev(-1))

        def b_start(self):
            self.send(0, 0, hop(-1), zdev(1))
            self.send(0, 0, hop(1), zdev(-1))
            self.b_x(0)

        def b_ring(self, i):
            if i == 4:
                self.got(4, 0, hop(4))
                self.b_x(4)
                return
            self.got(-i, 0, hop(-i))
            self.got(i, 0, hop(i))
            if i < 3:
                self.send(-i, 0, hop(-i - 1), zdev(1))
                self.send(i, 0, hop(i + 1), zdev(-1))
            else:
                self.send(-3 * self.way, 0, hop(4), zdev(self.way))
            self.b_x(-i)
            self.b_x(i)

        def b_pass(self, *rows):
            for d in rows:
                e = 3 if d % 2 == 0 else 1
                self.got(d, e, self.b_at(d, e))
                self.send(d, e, self.b_at(d, 2), xdev(1 if e == 3 else -1))

        def b_end(self):
            for d in (0, 1, -1, 2, -2, 3, -3, 4):
                e = 1 if d % 2 == 0 else 3
                self.got(d, e, self.b_at(d, e))
            for d in (0, 1, -1, 2, -2, 3, -3, 4):
                self.got(d, 2, self.b_at(d, 2))

        def end(self):
            cores(self.a_end, self.b_end)

    def cores(zero, one):
        pl.when(k == 0)(lambda: zero() and None)
        pl.when(k == 1)(lambda: one() and None)

    R = Gather(rall, r_out, r_in, 1)
    S = Gather(sall, s_out, s_in, -1)

    def weights_sent():
        remote(rall.at[0:31], rall.at[0:31], r_out.at[0], r_out.at[0], sibling).wait_send()
        remote(sall.at[0:31], sall.at[0:31], s_out.at[0], s_out.at[0], sibling).wait_send()

    leaving.append(weights_sent)

    def pump(n):
        cores(
            [
                lambda: (R.a_start(), S.a_start()),
                lambda: (R.a_z(1), R.a_z(3), R.a_z(2)),
                lambda: (R.a_ring(1, 0), S.a_z(1), S.a_z(3)),
                lambda: (R.a_ring(1, 1, 3, 2), S.a_z(2)),
                lambda: (R.a_ring(2, 0), S.a_ring(1, 0)),
                lambda: (R.a_ring(2, 1, 3, 2), S.a_ring(1, 1)),
                lambda: (R.a_ring(3, 0), S.a_ring(1, 3, 2)),
                lambda: (R.a_ring(3, 1, 3, 2), S.a_ring(2, 0)),
                lambda: S.a_ring(2, 1, 3),
                lambda: S.a_ring(2, 2),
                lambda: S.a_ring(3, 0),
                lambda: S.a_ring(3, 1, 3),
                lambda: S.a_ring(3, 2),
            ][n],
            [
                lambda: (R.b_start(), S.b_start()),
                lambda: R.b_ring(1),
                lambda: (R.b_ring(2), S.b_ring(1)),
                lambda: (R.b_ring(3), R.b_pass(0)),
                lambda: (S.b_ring(2), R.b_ring(4), R.b_pass(1, -1)),
                lambda: (R.b_pass(2, -2), S.b_pass(0)),
                lambda: (R.b_pass(3, -3, 4), S.b_ring(3)),
                lambda: (S.b_pass(1, -1), S.b_ring(4)),
                lambda: S.b_pass(2),
                lambda: S.b_pass(-2),
                lambda: S.b_pass(3),
                lambda: S.b_pass(-3, 4),
                lambda: None,
            ][n],
        )

    pump(0)
    start(remote(cot_h, cotb.at[k], cot_sem.at[0], cot_sem.at[1], sibling))
    coming["cot"] = remote(cot_h, cotb.at[1 - k], cot_sem.at[0], cot_sem.at[1], sibling).wait_recv
    cell = iota((256, 256), 0)
    cy, cx = cell >> 4, cell & 15
    inside = jnp.logical_and(
        jnp.logical_and(cy >= 1, cy <= 14), jnp.logical_and(cx >= 1, cx <= 14)
    )
    bm[...] = jnp.where(inside, 1.0, 0.0)
    into = select(padded_place(iota((256, 196), 1)) == iota((256, 196), 0))
    channel = iota((144, 48), 0)
    spread = select(channel - 48 * third(channel) == iota((144, 48), 1))
    same_group = third(iota((144, 144), 0)) == third(iota((144, 144), 1))
    blank = jnp.zeros((112, 196), BF)

    def centre(f):
        if f == 0:
            local[2].wait()
        return mmt(into, jnp.concatenate([feat[f], blank], axis=0))

    def put_shifts(f, value):
        xs[0, f, 16:272, :] = pltpu.roll(value, 1, 0).astype(BF)
        xs[1, f, 16:272, :] = value.astype(BF)
        xs[2, f, 16:272, :] = pltpu.roll(value, 255, 0).astype(BF)

    for f in range(2):
        for j in range(3):
            xs[j, f, 0:16, :] = jnp.zeros((16, 256), BF)
            xs[j, f, 272:288, :] = jnp.zeros((16, 256), BF)
        put_shifts(f, centre(f))
        pump(1 + f)
    local[3].wait()
    for tap in range(9):
        wc[tap] = jnp.zeros((256, 256), BF)
        dense = jnp.where(same_group, mm(spread, gk[tap]), 0.0)
        wc[tap, 0:144, 0:144] = dense.astype(BF)
        if tap == 4:
            pump(3)
    sqoe[144:256, :] = jnp.zeros((112, 288), BF)
    sqie[144:256, :] = jnp.zeros((112, 288), BF)
    pbuf[...] = jnp.zeros((8, 256), F32)
    pump(4)

    both = jnp.zeros((512, 256), F32)
    for dy in range(3):
        for dx in range(3):
            window = xs[dx, :, 16 * dy : 16 * dy + 256, :].reshape(512, 256)
            both = both + mmt(window, wc[3 * dy + dx])
        pump(5 + dy)
    for f in range(2):
        total = both[256 * f : 256 * f + 256]
        cv[f] = total
        act = total * sigmoid(total) * bm[...]
        ac[f] = act
        pbuf[f : f + 1, :] = jnp.sum(act, axis=0, keepdims=True) * (1.0 / 196.0)
    local[5].wait()
    local[6].wait()

    def put_sums(slots, sums, which):
        slots[t] = jnp.zeros((1, 768), F32)
        slots[t, :, 0:288] = sums[0:1]
        slots[t, :, 384:672] = sums[1:2]
        return exchange(lambda o: slots.at[t], slots, t, which)

    def get_sums(slots):
        both_rows = jnp.sum(slots[...], axis=0)
        return jnp.concatenate([both_rows[:, 0:288], both_rows[:, 384:672], jnp.zeros((6, 288), F32)], axis=0)

    coming["ps"] = put_sums(psl, exact(mm, pbuf[...], sqie[...]), 0)
    pump(8)

    clips = fclip[...].astype(F32)
    lane = iota((64, 128), 1)
    clip_col = jnp.sum(jnp.where(lane == 2 * token_at(iota((64, 128), 0)), clips, 0.0), axis=1, keepdims=True)
    before = jnp.logical_and((lane & 1) == 0, clips < clip_col)
    first = jnp.sum(jnp.where(before, 1.0, 0.0), axis=1, keepdims=True)
    lane16 = iota((64, 16), 1).astype(F32)
    kept = jnp.sum(jnp.where(lane16 == clip_col, keep[...].astype(F32), 0.0), axis=1, keepdims=True)
    place = (token_at(iota((64, 1), 0)).astype(F32) - first) * 64.0

    def live(d):
        return jnp.where(place + jnp.asarray(d, jnp.int32).astype(F32) < kept, 1.0, 0.0)

    lane1 = iota((1, 128), 1)

    def pair_mask(c):
        now = jnp.sum(jnp.where(lane1 == 2 * c, clips, 0.0), axis=1, keepdims=True)
        was = jnp.sum(jnp.where(lane1 == 2 * c - 1, clips, 0.0), axis=1, keepdims=True)
        return jnp.where(jnp.logical_and(now == was, iota((1, 1), 0) + c > 0), 1.0, 0.0)

    mask0, mask1 = pair_mask(2 * m), pair_mask(2 * m + 1)

    for f in range(2):
        sl[f] = slope(cv[f]) * bm[...]
        pump(9 + f)

    arrive("ps")
    squeezed = get_sums(psl)
    excite = sigmoid(exact(mmt, squeezed * sigmoid(squeezed), sqoe[...]))
    other = pl.ds(pl.multiple_of(64 * (1 - k), 64), 64)
    gather = select(patch_place(iota((256, 256), 0)) == iota((256, 256), 1))
    for f in range(2):
        hidden = xs[1, f, 16:272, :].astype(F32) + ac[f] * excite[f : f + 1, :]
        taps = mm(gather, hidden.astype(BF))
        base = 4 * (1 - f)
        rest = jnp.zeros((64, 128), F32)
        for s in range(4):
            tail = taps[64 * s : 64 * s + 64, 128:256]
            by = 16 * (s + base)
            rest = rest + (tail if by == 0 else pltpu.roll(tail, by, 1))
        main = taps[:, 0:128].astype(BF)
        if f == 0:
            mine = pl.ds(pl.multiple_of(64 * k, 64), 64)
            p1[mine, 0:128] = rest.astype(BF)
            for s in range(4):
                p1[mine, 128 * (s + 1) : 128 * (s + 2)] = main[64 * s : 64 * s + 64]
            start(remote(p1.at[mine], p1.at[mine], e_sem.at[0], e_sem.at[1], sibling))
            coming["even"] = lambda: remote(p1.at[other], p1.at[other], e_sem.at[0], e_sem.at[1], sibling).wait_recv()
        else:
            obuf[:, 512:640] = rest.astype(BF)
            for s in range(4):
                obuf[:, 128 * s : 128 * (s + 1)] = main[64 * s : 64 * s + 64]

    def send_odd():
        @pl.when(k == 0)
        def _():
            p0[64:128, :] = obuf[...]
            remote(obuf, p0.at[64:128], o_s.at[0], o_r.at[1], sibling).start()

        @pl.when(k == 1)
        def _():
            remote(obuf, p0.at[0:64], o_s.at[0], o_r.at[0], chip(m + 1, 1)).start()
            remote(obuf, p0.at[0:64], o_s.at[1], o_r.at[0], chip(m + 1, 0)).start()

    def odd_sent():
        remote(obuf, p0.at[0:64], o_s.at[0], o_r.at[0], sibling).wait_send()

        @pl.when(k == 1)
        def _():
            remote(obuf, p0.at[0:64], o_s.at[1], o_r.at[0], sibling).wait_send()

    def odd_here():
        remote(obuf, p0.at[0:64], o_s.at[0], o_r.at[0], sibling).wait_recv()

        @pl.when(k == 1)
        def _():
            remote(obuf, p0.at[64:128], o_s.at[0], o_r.at[1], sibling).wait_recv()

    send_odd()
    leaving.append(odd_sent)
    coming["odd"] = odd_here

    local[4].wait()
    R.end()
    fta[...] = rall[:, :, 1024:1152].reshape(512, 128).astype(F32)
    for p in range(8):
        rrest[0:64, 128 * p : 128 * p + 128] = fta[pl.ds(p, 64, stride=8), :].astype(BF)
    rrest[64:128, :] = jnp.zeros((64, 1024), BF)
    arrive("cot")
    order = select(token_at(iota((64, 64), 0)) == iota((64, 64), 1))
    back = jnp.concatenate([mm(order, cotb[0]).astype(BF), mm(order, cotb[1]).astype(BF)], axis=0)
    alive = jnp.concatenate([live(2 * m), live(2 * m + 1)], axis=0)
    gap[:, :, 0:512] = (
        (mmt(back, rall[:, :, 0:1024].reshape(512, 1024)) * alive).astype(BF).reshape(8, 16, 512)
    )
    pump(11)
    gap[:, :, 512:640] = (mmt(back, rrest[...]) * alive).astype(BF).reshape(8, 16, 128)

    def scattered(parts, chunk, slots):
        total = parts[chunk].astype(F32)
        for d in range(1, NT):
            total = total + slots[lax.rem(t + d, NT)].astype(F32)
        return total

    coming["rg"] = exchange(lambda o: gap.at[decoder_chunk(o)], rsg, t, 1)
    pump(12)

    def put_rows(src, value, dst, which):
        for i in range(16):
            src[i] = value[i : i + 1, :]

        @pl.when(is_self == 1)
        def _():
            dst[row_slot] = src[row_slot]

        @pl.when(is_self == 0)
        def _():
            i = trade[0]
            remote(src.at[i], dst.at[row_slot], pair.at[which, 0], pair.at[which, 1], row_dev(i)).start()

        for i in [trade[j] for j in (10, 6, 14, 2, 9, 11, 5, 7, 13, 15, 1, 3, 8, 4, 12)]:
            remote(src.at[i], dst.at[row_slot], pair.at[which, 0], pair.at[which, 1], row_dev(i)).start()

        def both(wait):
            @pl.when(is_self == 1)
            def _():
                wait(remote(src.at[0:15], dst.at[0:15], pair.at[which, 0], pair.at[which, 1], sibling))

            @pl.when(is_self == 0)
            def _():
                wait(remote(src, dst, pair.at[which, 0], pair.at[which, 1], sibling))

        leaving.append(lambda: both(lambda copy: copy.wait_send()))
        return lambda: both(lambda copy: copy.wait_recv())

    def get_rows(dst):
        return jnp.concatenate([dst[i] for i in range(16)], axis=0)

    arrive("even", "odd")
    S.end()
    fta[...] = sall[:, :, 1152:1280].reshape(512, 128).astype(F32)
    ftb[...] = sall[:, :, 1280:1408].reshape(512, 128).astype(F32)
    rest = jnp.zeros((64, 128), F32)
    for s in range(8):
        srest[0:64, SLOT[s] : SLOT[s] + 128] = fta[pl.ds(s, 64, stride=8), :].astype(BF)
        tail = ftb[pl.ds(s, 64, stride=8), :]
        rest = rest + (tail if s == 0 else pltpu.roll(tail, 16 * s, 1))
    srest[0:64, 512:640] = rest.astype(BF)
    srest[64:128, :] = jnp.zeros((64, 1152), BF)

    mask_col = jnp.concatenate(
        [jnp.broadcast_to(mask0, (64, 1)), jnp.broadcast_to(mask1, (64, 1))], axis=0
    )

    def pre_part(w0, w1):
        return mmt(p0[...], w0) * mask_col + mmt(p1[...], w1)

    prep[:, :, 0:512] = (
        pre_part(sall[:, :, 0:640].reshape(512, 640), sall[:, :, 512:1152].reshape(512, 640))
        .astype(BF)
        .reshape(8, 16, 512)
    )
    prep[:, :, 512:640] = pre_part(srest[:, 0:640], srest[:, 512:1152]).astype(BF).reshape(8, 16, 128)
    coming["rp"] = exchange(lambda o: prep.at[frame_chunk(o)], rsp, t, 2)

    arrive("rg")
    coming["ga"] = put_rows(gas, scattered(gap, decoder_chunk(t), rsg), gad, 3)
    arrive("rp")
    pre = scattered(prep, frame_chunk(t), rsp)
    pre_slope = slope(pre)
    arrive("ga")
    in_frames = frame_chunk(t)
    gpf[in_frames] = (get_rows(gad) * pre_slope).astype(BF)
    coming["gp"] = exchange(lambda o: gpf.at[in_frames], gpf, in_frames, 5)
    coming["aa"] = put_rows(acs, (pre * sigmoid(pre)).astype(BF).astype(F32), acd, 4)
    arrive("gp")
    grads = gpf[...].reshape(128, 640)
    def grad_taps(lanes):
        gpt[:, lanes] = mm(grads[:, 0:512], sall[:, :, lanes].reshape(512, lanes.stop - lanes.start)) + mm(grads[:, 512:640], srest[:, lanes])

    grad_taps(slice(0, 640))
    gos[0] = (gpt[0:64, 0:640] * mask0).astype(BF)
    start(remote(gos.at[0], gor.at[k], go_s.at[0], go_r.at[k], chip(m - 1, 1)))
    gos[1] = (gpt[64:128, 0:640] * mask1).astype(BF)

    @pl.when(k == 1)
    def _():
        remote(gos.at[1], gor.at[1], go_s.at[1], go_r.at[1], sibling).start()

    @pl.when(k == 0)
    def _():
        gor[0] = gos[1]

    def grad_odd_sent():
        @pl.when(k == 1)
        def _():
            remote(gos.at[1], gor.at[1], go_s.at[1], go_r.at[1], sibling).wait_send()

    def grad_odd_here():
        remote(gos.at[0], gor.at[1], go_s.at[0], go_r.at[1], sibling).wait_recv()

        @pl.when(k == 1)
        def _():
            remote(gos.at[0], gor.at[0], go_s.at[0], go_r.at[0], sibling).wait_recv()

    leaving.append(grad_odd_sent)
    grad_taps(slice(640, 1152))
    ges[...] = gpt[other, 512:1152].astype(BF)
    start(remote(ges, ger, ge_sem.at[0], ge_sem.at[1], sibling))
    coming["ge"] = remote(ges, ger, ge_sem.at[0], ge_sem.at[1], sibling).wait_recv
    coming["go"] = grad_odd_here

    arrive("aa")
    in_decoder = decoder_chunk(t)
    acf[in_decoder] = get_rows(acd).astype(BF)
    coming["af"] = exchange(lambda o: acf.at[in_decoder], acf, in_decoder, 6)

    ungather = select(patch_place(iota((256, 256), 1)) == iota((256, 256), 0))
    arrive("ge", "go")
    mine = pl.ds(pl.multiple_of(64 * k, 64), 64)
    even = gpt[mine, 512:1152] + ger[...].astype(F32)
    odd = gor[0].astype(F32) + gor[1].astype(F32)
    narrow = iota((64, 128), 1) < 16
    for f in range(2):
        if f == 0:
            tile, mains, base = even[:, 0:128], even[:, 128:640], 4
        else:
            tile, mains, base = odd[:, 512:640], odd[:, 0:512], 0
        main = jnp.concatenate([mains[:, 128 * s : 128 * s + 128] for s in range(4)], axis=0)
        tails = []
        for s in range(4):
            by = (128 - 16 * (s + base)) % 128
            tails.append(jnp.where(narrow, tile if by == 0 else pltpu.roll(tile, by, 1), 0.0))
        taps = jnp.concatenate([main, jnp.concatenate(tails, axis=0)], axis=1)
        top = taps.astype(BF)
        bottom = (taps - top.astype(F32)).astype(BF)
        grad = (mm(ungather, top) + mm(ungather, bottom)) * bm[...]
        gh[f] = grad
        pbuf[f : f + 1, :] = jnp.sum(grad * ac[f], axis=0, keepdims=True)

    inner = pbuf[...] * excite * (1.0 - excite)
    coming["pq"] = put_sums(psl2, exact(mm, inner, sqoe[...]), 7)
    arrive("af")
    acts = acf[...].reshape(128, 640)
    part = mm(acts[:, 0:512], rall[:, :, 0:1024].reshape(512, 1024)) + mm(acts[:, 512:640], rrest[...])
    low, high = part[0:64], part[64:128]
    kf = k.astype(F32)
    tks[...] = (low * kf + high * (1.0 - kf)).astype(BF)
    start(remote(tks, tkr, tk_sem.at[0], tk_sem.at[1], sibling))
    own_tokens = low * (1.0 - kf) + high * kf
    coming["tk"] = remote(tks, tkr, tk_sem.at[0], tk_sem.at[1], sibling).wait_recv

    outof = select(padded_place(iota((196, 256), 0)) == iota((196, 256), 1))
    natural = select(token_at(iota((64, 64), 1)) == iota((64, 64), 0))
    squeezed_slope = slope(squeezed)
    arrive("pq")
    grad_squeezed = get_sums(psl2) * squeezed_slope
    grad_pooled = exact(mmt, grad_squeezed, sqie[...]) * (1.0 / 196.0)
    for f in range(2):
        grad_active = gh[f] * excite[f : f + 1, :] + grad_pooled[f : f + 1, :]
        put_shifts(f, grad_active * sl[f])
    both = gh[...].reshape(512, 256)
    for dy in range(3):
        for dx in range(3):
            window = xs[2 - dx, :, 16 * (2 - dy) : 16 * (2 - dy) + 256, :].reshape(512, 256)
            both = both + mm(window, wc[3 * dy + dx])
    for f in range(2):
        turned = both[256 * f : 256 * f + 256].T[0:144].astype(BF)
        gout[f] = mmt(turned, outof).astype(BF)

    arrive("tk")
    rows = ((own_tokens + tkr[...].astype(F32)) * live(ctx)).astype(BF)
    llm[...] = mm(natural, rows).astype(BF)
    finish()


def per_device(features, group_kernel, squeeze_in, squeeze_out, sampler_kernel, readout_kernel, frame_clip, clip_keep, token_cotangent):
    V = pltpu.VMEM
    dma = pltpu.SemaphoreType.DMA
    scratch = [
        V((2, 144, 196), BF),
        V((9, 48, 144), BF),
        V((144, 144), BF),
        V((18, 1024), BF),
        V((32, 16, 1408), BF),
        V((32, 16, 1152), BF),
        V((128, 1152), BF),
        V((128, 1024), BF),
        V((512, 128), F32),
        V((512, 128), F32),
        V((2, 64, 1024), BF),
        V((9, 256, 256), BF),
        V((3, 2, 288, 256), BF),
        V((2, 256, 256), F32),
        V((2, 256, 256), F32),
        V((2, 256, 256), F32),
        V((256, 256), F32),
        V((2, 256, 256), F32),
        V((256, 288), BF),
        V((256, 288), BF),
        V((8, 256), F32),
        V((NT, 1, 768), F32),
        V((NT, 1, 768), F32),
        V((128, 640), BF),
        V((128, 640), BF),
        V((64, 640), BF),
        V((8, 16, 640), BF),
        V((8, 16, 640), BF),
        V((8, 16, 640), BF),
        V((8, 16, 640), BF),
        V((16, 1, 640), F32),
        V((16, 1, 640), F32),
        V((16, 1, 640), F32),
        V((16, 1, 640), F32),
        V((8, 16, 640), BF),
        V((8, 16, 640), BF),
        V((128, 1152), F32),
        V((64, 640), BF),
        V((64, 640), BF),
        V((2, 64, 640), BF),
        V((2, 64, 640), BF),
        V((64, 1024), BF),
        V((64, 1024), BF),
        dma((7,)),
        dma((2,)),
        dma((1,)), dma((32,)),
        dma((1,)), dma((32,)),
        dma((8, 2)),
        dma((2,)),
        dma((2,)), dma((2,)),
        dma((2,)),
        dma((2,)), dma((2,)),
        dma((2,)),
    ]
    spec = pl.BlockSpec(memory_space=pltpu.VMEM)
    hbm = pl.BlockSpec(memory_space=pltpu.HBM)
    llm_tokens, grad_features = pl.pallas_call(
        kernel,
        out_shape=(jax.ShapeDtypeStruct((64, 1024), BF), jax.ShapeDtypeStruct((2, 144, 196), BF)),
        in_specs=[hbm] * 6 + [spec] * 2 + [hbm],
        out_specs=(spec, spec),
        scratch_shapes=scratch,
        compiler_params=pltpu.CompilerParams(
            collective_id=0, has_side_effects=True, vmem_limit_bytes=62 * 1024 * 1024
        ),
        cost_estimate=pl.CostEstimate(flops=3_000_000_000, bytes_accessed=1_000_000, transcendentals=1_000_000),
        name="connector",
    )(
        features.transpose(0, 2, 1),
        group_kernel.transpose(0, 2, 1),
        squeeze_in,
        squeeze_out.T,
        sampler_kernel.reshape(144, 144),
        readout_kernel,
        frame_clip.reshape(1, 128),
        clip_keep.reshape(1, 16),
        token_cotangent,
    )
    return llm_tokens, grad_features.transpose(0, 2, 1)


def solution(mesh):
    placed = (
        P("ctx", None, "tp"),
        P(None, "tp", None),
        P("tp", None),
        P(None, "tp"),
        P("ctx", None, "tp"),
        P("ctx", "tp"),
        P(),
        P(),
        P("ctx", "tp"),
    )
    return jax.shard_map(
        per_device,
        mesh=mesh,
        in_specs=placed,
        out_specs=(P("ctx", "tp"), P("ctx", None, "tp")),
        check_vma=False,
    )
```

```python
import jax
import jax.numpy as jnp
from jax import lax
from jax.experimental import pallas as pl
from jax.experimental.pallas import tpu as pltpu
from jax.sharding import PartitionSpec as P

NX, NZ, NT = 4, 8, 8
BF = jnp.bfloat16
F32 = jnp.float32
MESH = pl.DeviceIdType.MESH
SLOT = (0, 128, 256, 384, 640, 768, 896, 1024)


def iota(shape, dim):
    return lax.broadcasted_iota(jnp.int32, shape, dim)


def select(hit):
    return jnp.where(hit, 1.0, 0.0).astype(BF)


def mm(a, b):
    return jnp.dot(a, b, preferred_element_type=F32)


def mmt(a, b):
    return lax.dot_general(a, b, (((1,), (1,)), ((), ())), preferred_element_type=F32)


def exact(dot, value, weight):
    high = value.astype(BF)
    left = value - high.astype(F32)
    middle = left.astype(BF)
    low = (left - middle.astype(F32)).astype(BF)
    return dot(high, weight) + (dot(middle, weight) + dot(low, weight))


def sigmoid(v):
    return jax.nn.sigmoid(v)


def slope(v):
    s = sigmoid(v)
    return s * (1.0 + v * (1.0 - s))


def padded_place(cell):
    row = (cell * 4682) >> 16
    return (row + 1) * 16 + (cell - 14 * row) + 1


def token_at(row):
    return 4 * (row & 15) + 2 * ((row >> 4) & 1) + ((row >> 5) & 1)


def patch_place(r):
    s = r >> 6
    token = token_at(r & 63)
    a = token >> 3
    b = token & 7
    return (2 * a + (s >> 1)) * 16 + 2 * b + (s & 1)


def third(v):
    return (v >= 48).astype(jnp.int32) + (v >= 96).astype(jnp.int32)


def kernel(
    feat_h, gk_h, sqi_h, sqo_h, samp_h, read_h, fclip, keep, cot_h,
    llm, gout,
    feat, gk, samp, read,
    sall, rall, srest, rrest, fta, ftb, cotb, wc, xs, cv, ac, sl, bm, gh, sqie, sqoe, pbuf, psl, psl2,
    p0, p1, obuf, prep, rsp, gap, rsg, gas, gad, acs, acd, gpf, acf, gpt, ges, ger, gos, gor, tks, tkr,
    load, cot_sem, s_out, s_in, r_out, r_in, pair, e_sem, o_s, o_r, ge_sem, go_s, go_r, tk_sem,
):
    ctx = lax.axis_index("ctx")
    t = lax.axis_index("tp")
    k = lax.rem(ctx, 2)
    m = lax.div(ctx, 2)
    z = lax.rem(m, NZ)
    x = lax.div(m, NZ)
    chips = NX * NZ

    def dev(xx, zz, kk, tt):
        return ((xx * NZ + zz) * 2 + kk, tt)

    def chip(mm_, kk):
        return (lax.rem(mm_ + chips, chips) * 2 + kk, t)

    def zdev(d):
        return dev(x, lax.rem(z + d + NZ, NZ), k, t)

    def xdev(d):
        return dev(lax.rem(x + d + NX, NX), z, k, t)

    def tdev(d):
        return (ctx, lax.rem(t + d, NT))

    sibling = (m * 2 + (1 - k), t)
    twist = lax.rem(m + lax.div(t, 4), 2)
    row_slot = lax.div(m, 2)
    is_self = (t < 4).astype(jnp.int32)

    def frame_chunk(o):
        return 4 * lax.rem(o, 2) + 2 * lax.rem(lax.div(o, 2), 2) + lax.rem(lax.div(o, 4) + m, 2)

    def decoder_chunk(o):
        return 4 * lax.rem(lax.div(o, 2), 2) + 2 * lax.rem(o, 2) + lax.rem(lax.div(o, 4) + m, 2)

    def row_dev(i):
        return ((2 * i + twist) * 2 + k, t)

    def remote(src, dst, send, recv, where):
        return pltpu.make_async_remote_copy(
            src_ref=src, dst_ref=dst, send_sem=send, recv_sem=recv, device_id=where, device_id_type=MESH
        )

    def exchange(source, slots, slot, which):
        for d in (4, 3, 5, 2, 6, 1, 7):
            o = lax.rem(t + d, NT)
            remote(source(o), slots.at[slot], pair.at[which, 0], pair.at[which, 1], tdev(d)).start()
        all_of = remote(slots.at[0 : NT - 1], slots.at[0 : NT - 1], pair.at[which, 0], pair.at[which, 1], tdev(1))
        leaving.append(all_of.wait_send)
        return all_of.wait_recv

    leaving = []
    coming = {}

    def start(copy):
        copy.start()
        leaving.append(copy.wait_send)

    def arrive(*names):
        for name in names:
            coming.pop(name)()

    def finish():
        arrive(*list(coming))
        for left in leaving:
            left()

    barrier = pltpu.get_barrier_semaphore()

    def hello(where):
        pl.semaphore_signal(barrier, inc=1, device_id=where, device_id_type=MESH)

    local = []
    for i, (src, dst) in enumerate(
        (
            (read_h, read), (samp_h, samp), (feat_h, feat), (gk_h, gk), (cot_h, cotb.at[k]),
            (sqi_h, sqie.at[0:144]), (sqo_h, sqoe.at[0:144]),
        )
    ):
        local.append(pltpu.make_async_copy(src, dst, load.at[i]))
        local[-1].start()

    trade = [lax.rem(row_slot + j, 16) for j in range(16)]

    @pl.when(is_self == 0)
    def _():
        hello(row_dev(trade[0]))

    for j in (10, 6, 14, 2, 9, 11, 5, 7, 13, 15, 1, 3, 8, 4, 12):
        hello(row_dev(trade[j]))
    for d in (4, 3, 5, 2, 6, 1, 7):
        hello(tdev(d))
    for d in (2, 1, 3):
        hello(xdev(d))
    hello(zdev(1))
    hello(zdev(-1))
    hello(sibling)
    hello(chip(m - 1, 1))

    @pl.when(k == 1)
    def _():
        hello(chip(m + 1, 0))
        hello(chip(m + 1, 1))


    own = 4 * z + x
    local[0].wait()
    rall[own, :, 0:1024] = read[0:16, :]
    last = read[16:18, :].astype(F32)
    for j in range(2):
        for p in range(8):
            fta[256 + j * 8 + p : 257 + j * 8 + p, :] = last[j : j + 1, 128 * p : 128 * p + 128]
    rall[own, :, 1024:1152] = fta[256:272, :].astype(BF)
    local[1].wait()
    ftb[0:144, :] = jnp.zeros((144, 128), F32)
    fta[0:144, :] = samp[:, 0:128].astype(F32)
    ftb[0:144, 0:16] = samp[:, 128:144].astype(F32)
    rest = jnp.zeros((16, 128), F32)
    for s in range(8):
        sall[own, :, SLOT[s] : SLOT[s] + 128] = fta[pl.ds(s, 16, stride=8), :].astype(BF)
        tail = ftb[pl.ds(s, 16, stride=8), :]
        rest = rest + (tail if s == 0 else pltpu.roll(tail, 16 * s, 1))
    sall[own, :, 512:640] = rest.astype(BF)
    sall[own, :, 1152:1280] = fta[128:144, :].astype(BF)
    sall[own, :, 1280:1408] = ftb[128:144, :].astype(BF)

    pl.semaphore_wait(barrier, 1 + (NX - 1) + 2 + (NT - 1) + (1 + 2 * k) + 16 - is_self)

    def zi(d):
        return lax.rem(z + d + NZ, NZ)

    def xi(e):
        return lax.rem(x + e, NX)

    def hop(d):
        return {-1: 0, -2: 1, -3: 2, 1: 3, 2: 4, 3: 5, 4: 6}[d]

    class Gather:
        def __init__(self, ref, out, into, way):
            self.ref, self.out, self.into, self.way = ref, out, into, way

        def block(self, d, e):
            return self.ref.at[4 * zi(d) + xi(e)]

        def send(self, d, e, sem, where):
            remote(self.block(d, e), self.block(d, e), self.out.at[0], self.into.at[sem], where).start()

        def got(self, d, e, sem):
            remote(self.block(d, e), self.block(d, e), self.out.at[0], self.into.at[sem], sibling).wait_recv()

        def a_z(self, e):
            if e:
                self.got(0, e, e)
            self.send(0, e, 4 + 7 * e + hop(-1), zdev(1))
            self.send(0, e, 4 + 7 * e + hop(1), zdev(-1))

        def a_start(self):
            for e in (2, 1, 3):
                self.send(0, 0, (-e) % 4, xdev(e))
            self.a_z(0)

        def a_ring(self, i, *columns):
            for e in columns:
                at = 4 + 7 * e
                self.got(-i, e, at + hop(-i))
                self.got(i, e, at + hop(i))
                if i < 3:
                    self.send(-i, e, at + hop(-i - 1), zdev(1))
                    self.send(i, e, at + hop(i + 1), zdev(-1))
                else:
                    way = 1 if e % 2 == 0 else -1
                    self.send(-3 * way, e, at + hop(4), zdev(way))

        def a_end(self):
            for e in (0, 1, 3, 2):
                self.got(4, e, 4 + 7 * e + hop(4))

        def b_at(self, d, e):
            return 7 + 3 * (d % 8) + e - 1

        def b_x(self, d):
            self.send(d, 0, self.b_at(d, 3), xdev(1))
            self.send(d, 0, self.b_at(d, 1), xdev(-1))

        def b_start(self):
            self.send(0, 0, hop(-1), zdev(1))
            self.send(0, 0, hop(1), zdev(-1))
            self.b_x(0)

        def b_ring(self, i):
            if i == 4:
                self.got(4, 0, hop(4))
                self.b_x(4)
                return
            self.got(-i, 0, hop(-i))
            self.got(i, 0, hop(i))
            if i < 3:
                self.send(-i, 0, hop(-i - 1), zdev(1))
                self.send(i, 0, hop(i + 1), zdev(-1))
            else:
                self.send(-3 * self.way, 0, hop(4), zdev(self.way))
            self.b_x(-i)
            self.b_x(i)

        def b_pass(self, *rows):
            for d in rows:
                e = 3 if d % 2 == 0 else 1
                self.got(d, e, self.b_at(d, e))
                self.send(d, e, self.b_at(d, 2), xdev(1 if e == 3 else -1))

        def b_end(self):
            for d in (0, 1, -1, 2, -2, 3, -3, 4):
                e = 1 if d % 2 == 0 else 3
                self.got(d, e, self.b_at(d, e))
            for d in (0, 1, -1, 2, -2, 3, -3, 4):
                self.got(d, 2, self.b_at(d, 2))

        def end(self):
            cores(self.a_end, self.b_end)

    def cores(zero, one):
        pl.when(k == 0)(lambda: zero() and None)
        pl.when(k == 1)(lambda: one() and None)

    R = Gather(rall, r_out, r_in, 1)
    S = Gather(sall, s_out, s_in, -1)

    def weights_sent():
        remote(rall.at[0:31], rall.at[0:31], r_out.at[0], r_out.at[0], sibling).wait_send()
        remote(sall.at[0:31], sall.at[0:31], s_out.at[0], s_out.at[0], sibling).wait_send()

    leaving.append(weights_sent)

    def pump(n):
        cores(
            [
                lambda: (R.a_start(), S.a_start()),
                lambda: (R.a_z(1), R.a_z(3), R.a_z(2)),
                lambda: (R.a_ring(1, 0), S.a_z(1), S.a_z(3)),
                lambda: (R.a_ring(1, 1, 3, 2), S.a_z(2)),
                lambda: (R.a_ring(2, 0), S.a_ring(1, 0)),
                lambda: (R.a_ring(2, 1, 3, 2), S.a_ring(1, 1)),
                lambda: (R.a_ring(3, 0), S.a_ring(1, 3, 2)),
                lambda: (R.a_ring(3, 1, 3, 2), S.a_ring(2, 0)),
                lambda: S.a_ring(2, 1, 3),
                lambda: S.a_ring(2, 2),
                lambda: S.a_ring(3, 0),
                lambda: S.a_ring(3, 1, 3),
                lambda: S.a_ring(3, 2),
            ][n],
            [
                lambda: (R.b_start(), S.b_start()),
                lambda: R.b_ring(1),
                lambda: (R.b_ring(2), S.b_ring(1)),
                lambda: (R.b_ring(3), R.b_pass(0)),
                lambda: (S.b_ring(2), R.b_ring(4), R.b_pass(1, -1)),
                lambda: (R.b_pass(2, -2), S.b_pass(0)),
                lambda: (R.b_pass(3, -3, 4), S.b_ring(3)),
                lambda: (S.b_pass(1, -1), S.b_ring(4)),
                lambda: S.b_pass(2),
                lambda: S.b_pass(-2),
                lambda: S.b_pass(3),
                lambda: S.b_pass(-3, 4),
                lambda: None,
            ][n],
        )

    pump(0)
    start(remote(cot_h, cotb.at[k], cot_sem.at[0], cot_sem.at[1], sibling))
    coming["cot"] = remote(cot_h, cotb.at[1 - k], cot_sem.at[0], cot_sem.at[1], sibling).wait_recv
    cell = iota((256, 256), 0)
    cy, cx = cell >> 4, cell & 15
    inside = jnp.logical_and(
        jnp.logical_and(cy >= 1, cy <= 14), jnp.logical_and(cx >= 1, cx <= 14)
    )
    bm[...] = jnp.where(inside, 1.0, 0.0)
    into = select(padded_place(iota((256, 196), 1)) == iota((256, 196), 0))
    channel = iota((144, 48), 0)
    spread = select(channel - 48 * third(channel) == iota((144, 48), 1))
    same_group = third(iota((144, 144), 0)) == third(iota((144, 144), 1))
    blank = jnp.zeros((112, 196), BF)

    def centre(f):
        if f == 0:
            local[2].wait()
        return mmt(into, jnp.concatenate([feat[f], blank], axis=0))

    def put_shifts(f, value):
        xs[0, f, 16:272, :] = pltpu.roll(value, 1, 0).astype(BF)
        xs[1, f, 16:272, :] = value.astype(BF)
        xs[2, f, 16:272, :] = pltpu.roll(value, 255, 0).astype(BF)

    for f in range(2):
        for j in range(3):
            xs[j, f, 0:16, :] = jnp.zeros((16, 256), BF)
            xs[j, f, 272:288, :] = jnp.zeros((16, 256), BF)
        put_shifts(f, centre(f))
        pump(1 + f)
    local[3].wait()
    for tap in range(9):
        wc[tap] = jnp.zeros((256, 256), BF)
        dense = jnp.where(same_group, mm(spread, gk[tap]), 0.0)
        wc[tap, 0:144, 0:144] = dense.astype(BF)
        if tap == 4:
            pump(3)
    sqoe[144:256, :] = jnp.zeros((112, 288), BF)
    sqie[144:256, :] = jnp.zeros((112, 288), BF)
    pbuf[...] = jnp.zeros((8, 256), F32)
    pump(4)

    both = jnp.zeros((512, 256), F32)
    for dy in range(3):
        for dx in range(3):
            window = xs[dx, :, 16 * dy : 16 * dy + 256, :].reshape(512, 256)
            both = both + mmt(window, wc[3 * dy + dx])
        pump(5 + dy)
    for f in range(2):
        total = both[256 * f : 256 * f + 256]
        cv[f] = total
        act = total * sigmoid(total) * bm[...]
        ac[f] = act
        pbuf[f : f + 1, :] = jnp.sum(act, axis=0, keepdims=True) * (1.0 / 196.0)
    local[5].wait()
    local[6].wait()

    def put_sums(slots, sums, which):
        slots[t] = jnp.zeros((1, 768), F32)
        slots[t, :, 0:288] = sums[0:1]
        slots[t, :, 384:672] = sums[1:2]
        return exchange(lambda o: slots.at[t], slots, t, which)

    def get_sums(slots):
        both_rows = jnp.sum(slots[...], axis=0)
        return jnp.concatenate([both_rows[:, 0:288], both_rows[:, 384:672], jnp.zeros((6, 288), F32)], axis=0)

    coming["ps"] = put_sums(psl, exact(mm, pbuf[...], sqie[...]), 0)
    pump(8)

    clips = fclip[...].astype(F32)
    lane = iota((64, 128), 1)
    clip_col = jnp.sum(jnp.where(lane == 2 * token_at(iota((64, 128), 0)), clips, 0.0), axis=1, keepdims=True)
    before = jnp.logical_and((lane & 1) == 0, clips < clip_col)
    first = jnp.sum(jnp.where(before, 1.0, 0.0), axis=1, keepdims=True)
    lane16 = iota((64, 16), 1).astype(F32)
    kept = jnp.sum(jnp.where(lane16 == clip_col, keep[...].astype(F32), 0.0), axis=1, keepdims=True)
    place = (token_at(iota((64, 1), 0)).astype(F32) - first) * 64.0

    def live(d):
        return jnp.where(place + jnp.asarray(d, jnp.int32).astype(F32) < kept, 1.0, 0.0)

    lane1 = iota((1, 128), 1)

    def pair_mask(c):
        now = jnp.sum(jnp.where(lane1 == 2 * c, clips, 0.0), axis=1, keepdims=True)
        was = jnp.sum(jnp.where(lane1 == 2 * c - 1, clips, 0.0), axis=1, keepdims=True)
        return jnp.where(jnp.logical_and(now == was, iota((1, 1), 0) + c > 0), 1.0, 0.0)

    mask0, mask1 = pair_mask(2 * m), pair_mask(2 * m + 1)

    for f in range(2):
        sl[f] = slope(cv[f]) * bm[...]
        pump(9 + f)

    arrive("ps")
    squeezed = get_sums(psl)
    excite = sigmoid(exact(mmt, squeezed * sigmoid(squeezed), sqoe[...]))
    other = pl.ds(pl.multiple_of(64 * (1 - k), 64), 64)
    gather = select(patch_place(iota((256, 256), 0)) == iota((256, 256), 1))
    for f in range(2):
        hidden = xs[1, f, 16:272, :].astype(F32) + ac[f] * excite[f : f + 1, :]
        taps = mm(gather, hidden.astype(BF))
        base = 4 * (1 - f)
        rest = jnp.zeros((64, 128), F32)
        for s in range(4):
            tail = taps[64 * s : 64 * s + 64, 128:256]
            by = 16 * (s + base)
            rest = rest + (tail if by == 0 else pltpu.roll(tail, by, 1))
        main = taps[:, 0:128].astype(BF)
        if f == 0:
            mine = pl.ds(pl.multiple_of(64 * k, 64), 64)
            p1[mine, 0:128] = rest.astype(BF)
            for s in range(4):
                p1[mine, 128 * (s + 1) : 128 * (s + 2)] = main[64 * s : 64 * s + 64]
            start(remote(p1.at[mine], p1.at[mine], e_sem.at[0], e_sem.at[1], sibling))
            coming["even"] = lambda: remote(p1.at[other], p1.at[other], e_sem.at[0], e_sem.at[1], sibling).wait_recv()
        else:
            obuf[:, 512:640] = rest.astype(BF)
            for s in range(4):
                obuf[:, 128 * s : 128 * (s + 1)] = main[64 * s : 64 * s + 64]

    def send_odd():
        @pl.when(k == 0)
        def _():
            p0[64:128, :] = obuf[...]
            remote(obuf, p0.at[64:128], o_s.at[0], o_r.at[1], sibling).start()

        @pl.when(k == 1)
        def _():
            remote(obuf, p0.at[0:64], o_s.at[0], o_r.at[0], chip(m + 1, 1)).start()
            remote(obuf, p0.at[0:64], o_s.at[1], o_r.at[0], chip(m + 1, 0)).start()

    def odd_sent():
        remote(obuf, p0.at[0:64], o_s.at[0], o_r.at[0], sibling).wait_send()

        @pl.when(k == 1)
        def _():
            remote(obuf, p0.at[0:64], o_s.at[1], o_r.at[0], sibling).wait_send()

    def odd_here():
        remote(obuf, p0.at[0:64], o_s.at[0], o_r.at[0], sibling).wait_recv()

        @pl.when(k == 1)
        def _():
            remote(obuf, p0.at[64:128], o_s.at[0], o_r.at[1], sibling).wait_recv()

    send_odd()
    leaving.append(odd_sent)
    coming["odd"] = odd_here

    local[4].wait()
    R.end()
    fta[...] = rall[:, :, 1024:1152].reshape(512, 128).astype(F32)
    for p in range(8):
        rrest[0:64, 128 * p : 128 * p + 128] = fta[pl.ds(p, 64, stride=8), :].astype(BF)
    rrest[64:128, :] = jnp.zeros((64, 1024), BF)
    arrive("cot")
    order = select(token_at(iota((64, 64), 0)) == iota((64, 64), 1))
    back = jnp.concatenate([mm(order, cotb[0]).astype(BF), mm(order, cotb[1]).astype(BF)], axis=0)
    alive = jnp.concatenate([live(2 * m), live(2 * m + 1)], axis=0)
    gap[:, :, 0:512] = (
        (mmt(back, rall[:, :, 0:1024].reshape(512, 1024)) * alive).astype(BF).reshape(8, 16, 512)
    )
    pump(11)
    pump(12)
    gap[:, :, 512:640] = (mmt(back, rrest[...]) * alive).astype(BF).reshape(8, 16, 128)

    def scattered(parts, chunk, slots):
        total = parts[chunk].astype(F32)
        for d in range(1, NT):
            total = total + slots[lax.rem(t + d, NT)].astype(F32)
        return total

    coming["rg"] = exchange(lambda o: gap.at[decoder_chunk(o)], rsg, t, 1)

    def put_rows(src, value, dst, which):
        for i in range(16):
            src[i] = value[i : i + 1, :]

        @pl.when(is_self == 1)
        def _():
            dst[row_slot] = src[row_slot]

        @pl.when(is_self == 0)
        def _():
            i = trade[0]
            remote(src.at[i], dst.at[row_slot], pair.at[which, 0], pair.at[which, 1], row_dev(i)).start()

        for i in [trade[j] for j in (10, 6, 14, 2, 9, 11, 5, 7, 13, 15, 1, 3, 8, 4, 12)]:
            remote(src.at[i], dst.at[row_slot], pair.at[which, 0], pair.at[which, 1], row_dev(i)).start()

        def both(wait):
            @pl.when(is_self == 1)
            def _():
                wait(remote(src.at[0:15], dst.at[0:15], pair.at[which, 0], pair.at[which, 1], sibling))

            @pl.when(is_self == 0)
            def _():
                wait(remote(src, dst, pair.at[which, 0], pair.at[which, 1], sibling))

        leaving.append(lambda: both(lambda copy: copy.wait_send()))
        return lambda: both(lambda copy: copy.wait_recv())

    def get_rows(dst):
        return jnp.concatenate([dst[i] for i in range(16)], axis=0)

    arrive("even", "odd")
    S.end()
    fta[...] = sall[:, :, 1152:1280].reshape(512, 128).astype(F32)
    ftb[...] = sall[:, :, 1280:1408].reshape(512, 128).astype(F32)
    rest = jnp.zeros((64, 128), F32)
    for s in range(8):
        srest[0:64, SLOT[s] : SLOT[s] + 128] = fta[pl.ds(s, 64, stride=8), :].astype(BF)
        tail = ftb[pl.ds(s, 64, stride=8), :]
        rest = rest + (tail if s == 0 else pltpu.roll(tail, 16 * s, 1))
    srest[0:64, 512:640] = rest.astype(BF)
    srest[64:128, :] = jnp.zeros((64, 1152), BF)

    mask_col = jnp.concatenate(
        [jnp.broadcast_to(mask0, (64, 1)), jnp.broadcast_to(mask1, (64, 1))], axis=0
    )

    def pre_part(w0, w1):
        return mmt(p0[...], w0) * mask_col + mmt(p1[...], w1)

    prep[:, :, 0:512] = (
        pre_part(sall[:, :, 0:640].reshape(512, 640), sall[:, :, 512:1152].reshape(512, 640))
        .astype(BF)
        .reshape(8, 16, 512)
    )
    main_here = exchange(lambda o: prep.at[frame_chunk(o), :, 0:512], rsp.at[:, :, 0:512], t, 2)
    prep[:, :, 512:640] = pre_part(srest[:, 0:640], srest[:, 512:1152]).astype(BF).reshape(8, 16, 128)
    tail_here = exchange(lambda o: prep.at[frame_chunk(o), :, 512:640], rsp.at[:, :, 512:640], t, 8)
    coming["rp"] = lambda: (main_here(), tail_here())

    arrive("rg")
    coming["ga"] = put_rows(gas, scattered(gap, decoder_chunk(t), rsg), gad, 3)
    arrive("rp")
    pre = scattered(prep, frame_chunk(t), rsp)
    pre_slope = slope(pre)
    arrive("ga")
    in_frames = frame_chunk(t)
    gpf[in_frames] = (get_rows(gad) * pre_slope).astype(BF)
    coming["gp"] = exchange(lambda o: gpf.at[in_frames], gpf, in_frames, 5)
    coming["aa"] = put_rows(acs, (pre * sigmoid(pre)).astype(BF).astype(F32), acd, 4)
    arrive("gp")
    grads = gpf[...].reshape(128, 640)
    def grad_taps(lanes):
        gpt[:, lanes] = mm(grads[:, 0:512], sall[:, :, lanes].reshape(512, lanes.stop - lanes.start)) + mm(grads[:, 512:640], srest[:, lanes])

    grad_taps(slice(0, 640))
    gos[0] = (gpt[0:64, 0:640] * mask0).astype(BF)
    start(remote(gos.at[0], gor.at[k], go_s.at[0], go_r.at[k], chip(m - 1, 1)))
    gos[1] = (gpt[64:128, 0:640] * mask1).astype(BF)

    @pl.when(k == 1)
    def _():
        remote(gos.at[1], gor.at[1], go_s.at[1], go_r.at[1], sibling).start()

    @pl.when(k == 0)
    def _():
        gor[0] = gos[1]

    def grad_odd_sent():
        @pl.when(k == 1)
        def _():
            remote(gos.at[1], gor.at[1], go_s.at[1], go_r.at[1], sibling).wait_send()

    def grad_odd_here():
        remote(gos.at[0], gor.at[1], go_s.at[0], go_r.at[1], sibling).wait_recv()

        @pl.when(k == 1)
        def _():
            remote(gos.at[0], gor.at[0], go_s.at[0], go_r.at[0], sibling).wait_recv()

    leaving.append(grad_odd_sent)
    grad_taps(slice(640, 1152))
    ges[...] = gpt[other, 512:1152].astype(BF)
    start(remote(ges, ger, ge_sem.at[0], ge_sem.at[1], sibling))
    coming["ge"] = remote(ges, ger, ge_sem.at[0], ge_sem.at[1], sibling).wait_recv
    coming["go"] = grad_odd_here

    arrive("aa")
    in_decoder = decoder_chunk(t)
    acf[in_decoder] = get_rows(acd).astype(BF)
    coming["af"] = exchange(lambda o: acf.at[in_decoder], acf, in_decoder, 6)

    ungather = select(patch_place(iota((256, 256), 1)) == iota((256, 256), 0))
    arrive("ge", "go")
    mine = pl.ds(pl.multiple_of(64 * k, 64), 64)
    even = gpt[mine, 512:1152] + ger[...].astype(F32)
    odd = gor[0].astype(F32) + gor[1].astype(F32)
    narrow = iota((64, 128), 1) < 16
    for f in range(2):
        if f == 0:
            tile, mains, base = even[:, 0:128], even[:, 128:640], 4
        else:
            tile, mains, base = odd[:, 512:640], odd[:, 0:512], 0
        main = jnp.concatenate([mains[:, 128 * s : 128 * s + 128] for s in range(4)], axis=0)
        tails = []
        for s in range(4):
            by = (128 - 16 * (s + base)) % 128
            tails.append(jnp.where(narrow, tile if by == 0 else pltpu.roll(tile, by, 1), 0.0))
        taps = jnp.concatenate([main, jnp.concatenate(tails, axis=0)], axis=1)
        top = taps.astype(BF)
        bottom = (taps - top.astype(F32)).astype(BF)
        grad = (mm(ungather, top) + mm(ungather, bottom)) * bm[...]
        gh[f] = grad
        pbuf[f : f + 1, :] = jnp.sum(grad * ac[f], axis=0, keepdims=True)

    inner = pbuf[...] * excite * (1.0 - excite)
    coming["pq"] = put_sums(psl2, exact(mm, inner, sqoe[...]), 7)
    arrive("af")
    acts = acf[...].reshape(128, 640)
    part = mm(acts[:, 0:512], rall[:, :, 0:1024].reshape(512, 1024)) + mm(acts[:, 512:640], rrest[...])
    low, high = part[0:64], part[64:128]
    kf = k.astype(F32)
    tks[...] = (low * kf + high * (1.0 - kf)).astype(BF)
    start(remote(tks, tkr, tk_sem.at[0], tk_sem.at[1], sibling))
    own_tokens = low * (1.0 - kf) + high * kf
    coming["tk"] = remote(tks, tkr, tk_sem.at[0], tk_sem.at[1], sibling).wait_recv

    outof = select(padded_place(iota((196, 256), 0)) == iota((196, 256), 1))
    natural = select(token_at(iota((64, 64), 1)) == iota((64, 64), 0))
    squeezed_slope = slope(squeezed)
    arrive("pq")
    grad_squeezed = get_sums(psl2) * squeezed_slope
    grad_pooled = exact(mmt, grad_squeezed, sqie[...]) * (1.0 / 196.0)
    for f in range(2):
        grad_active = gh[f] * excite[f : f + 1, :] + grad_pooled[f : f + 1, :]
        put_shifts(f, grad_active * sl[f])
    both = gh[...].reshape(512, 256)
    for dy in range(3):
        for dx in range(3):
            window = xs[2 - dx, :, 16 * (2 - dy) : 16 * (2 - dy) + 256, :].reshape(512, 256)
            both = both + mm(window, wc[3 * dy + dx])
    for f in range(2):
        turned = both[256 * f : 256 * f + 256].T[0:144].astype(BF)
        gout[f] = mmt(turned, outof).astype(BF)

    arrive("tk")
    rows = ((own_tokens + tkr[...].astype(F32)) * live(ctx)).astype(BF)
    llm[...] = mm(natural, rows).astype(BF)
    finish()


def per_device(features, group_kernel, squeeze_in, squeeze_out, sampler_kernel, readout_kernel, frame_clip, clip_keep, token_cotangent):
    V = pltpu.VMEM
    dma = pltpu.SemaphoreType.DMA
    scratch = [
        V((2, 144, 196), BF),
        V((9, 48, 144), BF),
        V((144, 144), BF),
        V((18, 1024), BF),
        V((32, 16, 1408), BF),
        V((32, 16, 1152), BF),
        V((128, 1152), BF),
        V((128, 1024), BF),
        V((512, 128), F32),
        V((512, 128), F32),
        V((2, 64, 1024), BF),
        V((9, 256, 256), BF),
        V((3, 2, 288, 256), BF),
        V((2, 256, 256), F32),
        V((2, 256, 256), F32),
        V((2, 256, 256), F32),
        V((256, 256), F32),
        V((2, 256, 256), F32),
        V((256, 288), BF),
        V((256, 288), BF),
        V((8, 256), F32),
        V((NT, 1, 768), F32),
        V((NT, 1, 768), F32),
        V((128, 640), BF),
        V((128, 640), BF),
        V((64, 640), BF),
        V((8, 16, 640), BF),
        V((8, 16, 640), BF),
        V((8, 16, 640), BF),
        V((8, 16, 640), BF),
        V((16, 1, 640), F32),
        V((16, 1, 640), F32),
        V((16, 1, 640), F32),
        V((16, 1, 640), F32),
        V((8, 16, 640), BF),
        V((8, 16, 640), BF),
        V((128, 1152), F32),
        V((64, 640), BF),
        V((64, 640), BF),
        V((2, 64, 640), BF),
        V((2, 64, 640), BF),
        V((64, 1024), BF),
        V((64, 1024), BF),
        dma((7,)),
        dma((2,)),
        dma((1,)), dma((32,)),
        dma((1,)), dma((32,)),
        dma((9, 2)),
        dma((2,)),
        dma((2,)), dma((2,)),
        dma((2,)),
        dma((2,)), dma((2,)),
        dma((2,)),
    ]
    spec = pl.BlockSpec(memory_space=pltpu.VMEM)
    hbm = pl.BlockSpec(memory_space=pltpu.HBM)
    llm_tokens, grad_features = pl.pallas_call(
        kernel,
        out_shape=(jax.ShapeDtypeStruct((64, 1024), BF), jax.ShapeDtypeStruct((2, 144, 196), BF)),
        in_specs=[hbm] * 6 + [spec] * 2 + [hbm],
        out_specs=(spec, spec),
        scratch_shapes=scratch,
        compiler_params=pltpu.CompilerParams(
            collective_id=0, has_side_effects=True, vmem_limit_bytes=62 * 1024 * 1024
        ),
        cost_estimate=pl.CostEstimate(flops=3_000_000_000, bytes_accessed=1_000_000, transcendentals=1_000_000),
        name="connector",
    )(
        features.transpose(0, 2, 1),
        group_kernel.transpose(0, 2, 1),
        squeeze_in,
        squeeze_out.T,
        sampler_kernel.reshape(144, 144),
        readout_kernel,
        frame_clip.reshape(1, 128),
        clip_keep.reshape(1, 16),
        token_cotangent,
    )
    return llm_tokens, grad_features.transpose(0, 2, 1)


def solution(mesh):
    placed = (
        P("ctx", None, "tp"),
        P(None, "tp", None),
        P("tp", None),
        P(None, "tp"),
        P("ctx", None, "tp"),
        P("ctx", "tp"),
        P(),
        P(),
        P("ctx", "tp"),
    )
    return jax.shard_map(
        per_device,
        mesh=mesh,
        in_specs=placed,
        out_specs=(P("ctx", "tp"), P("ctx", None, "tp")),
        check_vma=False,
    )
```
